128 devices in a mesh: patch: 32 (over y, x, core), slab: 4 (over z).
Axes of the slice: x: 4, y: 4, z: 4, core: 2. Of those that a mesh axis runs over, the one named last changes fastest.
Arguments:
- history: bfloat16 [512, 256, 128], P('patch', 'slab'), may hold values from -6 to 6
- interp_weights: bfloat16 [512, 32, 4], P('patch'), may hold values from -3 to 3
- pair_table: int32 [512, 32, 3], P('patch'), may hold values from 0 to 511, as said below
- coupling: bfloat16 [512, 32, 128, 128], P('patch', 'slab'), may hold values from -0.09375 to 0.09375
- self_inverse: bfloat16 [512, 128, 128], P('patch'), may hold values from -0.5 to 0.5
- incident: float32 [512, 4, 128], P('patch'), may hold values from -6 to 6
Outputs:
- amplitudes: bfloat16 [512, 4, 128], P('patch')
The draws below stay inside these ranges and needn't reach their ends.
Inputs may be any that keep to these rules, and one draw needn't show every extreme that they name: pair_table[p, k] holds the observer patch (0 to 511), the first delay step (1 to 252) and the band width (1 to 4) of the k-th interaction whose sources are patch p's.
All inputs are finite; a program needn't handle non-finite values.
Results may differ from the reference program's by a relative error of at most 0.008.
Values may be sent and summed in bfloat16 or wider, within the bound.
No kernel may reach another device: no remote copies, remote signals or barrier semaphores. Data moves between devices by JAX's collectives and lax.ppermute only.
A program may use at most 64 MiB of HBM per device.

```python
import jax
import jax.numpy as jnp
from jax import lax

SRC = 128
HIST = 256
WMAX = 4
STEPS = 4
PAIRS = 32
PATCHES = 512


def draw_pair_table(key, part):
    keys = jax.random.split(jax.random.fold_in(key, 7), 5)
    observer = jax.random.randint(keys[0], (PATCHES, PAIRS), 0, PATCHES)
    near_delay = jax.random.randint(keys[1], (PATCHES, PAIRS), 1, 2)
    far_delay = jax.random.randint(keys[2], (PATCHES, PAIRS), 1, HIST - WMAX + 1)
    picker = jax.random.randint(keys[3], (PATCHES, PAIRS), 0, 4)
    first_delay = jnp.where(picker == 0, near_delay, far_delay)
    band_width = jax.random.randint(keys[4], (PATCHES, PAIRS), 1, WMAX + 1)
    observer = observer.at[0, 0].set(PATCHES - 1)
    first_delay = first_delay.at[0, 1].set(HIST - WMAX)
    return jnp.stack([observer, first_delay, band_width], axis=-1).astype(jnp.int32)


def shard_levels(stream_key, shape, shards, smallest, largest):
    def one(axis_at, blocks):
        steps = jax.random.uniform(jax.random.fold_in(jax.random.fold_in(stream_key, 6), axis_at), (blocks,), jnp.float32, smallest / len(shards), largest / len(shards))
        return jnp.repeat(jnp.exp(steps), shape[axis_at] // blocks).reshape((-1,) + (1,) * (len(shape) - axis_at - 1))

    gain = one(*shards[0])
    for cut in shards[1:]:
        gain = gain * one(*cut)
    return gain


def bell_draw(stream_key, dims, deviation, limit, cuts=(), kind=jnp.bfloat16):
    level = shard_levels(stream_key, dims, cuts, -0.22, 0.18) if cuts else 1.0
    values = jax.random.normal(stream_key, dims, jnp.float32) * deviation * level
    return jnp.minimum(jnp.maximum(values, -limit), limit).astype(kind)


def setup_inputs(seed: int = 0) -> dict:
    seeds = jax.random.split(jax.random.key(seed), 7)
    return {
        "history": bell_draw(seeds[0], (PATCHES, HIST, SRC), 1.0, 6.0, ((0, 32), (1, 4))),
        "interp_weights": bell_draw(seeds[1], (PATCHES, PAIRS, WMAX), 1.0, 3.0, ((0, 32),)),
        "pair_table": draw_pair_table(jax.random.fold_in(seeds[6], 71), 0),
        "coupling": bell_draw(seeds[3], (PATCHES, PAIRS, SRC, SRC), (SRC * PAIRS) ** -0.5, 0.09375, ((0, 32), (1, 4))),
        "self_inverse": bell_draw(seeds[4], (PATCHES, SRC, SRC), SRC ** -0.5, 0.5, ((0, 32),)),
        "incident": bell_draw(seeds[5], (PATCHES, STEPS, SRC), 1.0, 6.0, ((0, 32),), jnp.float32),
    }


def reference(history, interp_weights, pair_table, coupling, self_inverse, incident):
    observer = pair_table[:, :, 0]
    first_delay = pair_table[:, :, 1]
    band_width = pair_table[:, :, 2]
    tap_index = jnp.arange(WMAX, dtype=jnp.int32)
    weights = jnp.where(tap_index[None, None, :] < band_width[:, :, None], interp_weights.astype(jnp.float32), jnp.float32(0.0))
    new_amps = jnp.zeros((PATCHES, STEPS, SRC), jnp.bfloat16)
    patch_rows = jnp.arange(PATCHES, dtype=jnp.int32)[:, None, None]
    for time_step in range(STEPS):
        timeline = jnp.concatenate([new_amps[:, ::-1], history], axis=1).astype(jnp.float32)
        position = (first_delay[:, :, None] + tap_index[None, None, :] - time_step - 1 + STEPS).astype(jnp.int32)
        picked = timeline[patch_rows, position]
        driven = jnp.sum(weights[..., None] * picked, axis=2).astype(jnp.bfloat16)

        def apply_one(pieces):
            matrices, vectors = pieces
            return jnp.einsum('kij,kj->ki', matrices.astype(jnp.float32), vectors.astype(jnp.float32))

        coupled = lax.map(apply_one, (coupling, driven))
        scattered = jax.ops.segment_sum(coupled.reshape(-1, SRC), observer.reshape(-1), num_segments=PATCHES)
        drive = (incident[:, time_step] - scattered).astype(jnp.bfloat16)
        amplitude = jnp.einsum('pij,pj->pi', self_inverse.astype(jnp.float32), drive.astype(jnp.float32)).astype(jnp.bfloat16)
        new_amps = new_amps.at[:, time_step].set(amplitude)
    return new_amps
```

```python
import jax
import jax.numpy as jnp
from jax import lax
from jax.experimental import pallas as pl
from jax.experimental.pallas import tpu as pltpu
from jax.sharding import PartitionSpec as P

WMAX = 4
STEPS = 4
LAGS = STEPS - 1

BF16 = jnp.bfloat16
F32 = jnp.float32


def dot_f32(a, b, contract):
    return lax.dot_general(a, b, (contract, ((), ())), preferred_element_type=F32)


def history_kernel(rows_ref, hist_ref, *outs):
    own_ref, send_refs = outs[0], outs[1:]
    patches, slab_len, src = hist_ref.shape
    slabs = len(send_refs) // 2 + 1
    pairs = rows_ref.shape[2] // STEPS
    local = pairs // slabs
    h = lax.broadcasted_iota(jnp.int32, (slab_len, STEPS * pairs), 0).astype(F32)
    for p in range(0, patches, 2):
        parts = []
        for q in (p, p + 1):
            j = h - rows_ref[q, 0:1, :]
            table = jnp.where(j == 0, rows_ref[q, 1:2, :], 0.0)
            for tap in range(1, WMAX):
                table = jnp.where(j == tap, rows_ref[q, tap + 1 : tap + 2, :], table)
            parts.append(dot_f32(table.astype(BF16), hist_ref[q], ((0,), (0,))))
        at = pl.ds(p * local, 2 * local)
        for n in range(STEPS):
            for s in range(slabs):
                lo = n * pairs + s * local
                both = jnp.concatenate([part[lo : lo + local] for part in parts], axis=0)
                if s == 0:
                    own_ref[n, at, :] = both
                elif n == 0:
                    send_refs[s - 1][0, at, :] = both.astype(BF16)
                else:
                    send_refs[slabs - 2 + s][n - 1, at, :] = both.astype(BF16)


def field_of(driven, obs_ref, coup_ref, send_ref):
    rows, src = driven.shape
    patches = coup_ref.shape[0]
    local = rows // patches
    row_id = lax.broadcasted_iota(jnp.int32, (local, src), 0)
    coupled = []
    for p in range(patches):
        mine = driven[p * local : (p + 1) * local].astype(BF16)
        full = dot_f32(mine, coup_ref[p].reshape(local * src, src), ((1,), (1,)))
        out = full[:, :src]
        for k in range(1, local):
            out = jnp.where(row_id == k, full[:, k * src : (k + 1) * src], out)
        coupled.append(out)
    coupled = jnp.concatenate(coupled, axis=0).astype(BF16)
    blocks, slabs, dev_rows, _ = send_ref.shape
    targets = lax.broadcasted_iota(jnp.int32, (blocks * dev_rows, rows), 0)
    onehot = jnp.where(targets == obs_ref[0:1, :], 1.0, 0.0).astype(BF16)
    field = dot_f32(onehot, coupled, ((1,), (0,))).astype(BF16)
    field = field.reshape(blocks, dev_rows, src)
    for s in range(slabs):
        send_ref[:, s] = field


def first_kernel(own_ref, a_ref, b_ref, c_ref, obs_ref, coup_ref, send_ref):
    driven = own_ref[0] + a_ref[0].astype(F32) + b_ref[0].astype(F32) + c_ref[0].astype(F32)
    field_of(driven, obs_ref, coup_ref, send_ref)


def amplitude_of(step, recv_ref, inc_ref, sinv_ref):
    sources, patches, src = recv_ref.shape
    total = jnp.sum(recv_ref[...].astype(F32), axis=0)
    drive = (inc_ref[step] - total).astype(BF16)
    row_id = lax.broadcasted_iota(jnp.int32, (patches, src), 0)
    amp = jnp.zeros((patches, src), F32)
    full = dot_f32(drive, sinv_ref[...].reshape(patches * src, src), ((1,), (1,)))
    for p in range(patches):
        amp = jnp.where(row_id == p, full[:, p * src : (p + 1) * src], amp)
    return amp.astype(BF16)


def step_kernel(step, recv_ref, inc_ref, sinv_ref, lag_ref, own_ref, a_ref, b_ref, c_ref, obs_ref, coup_ref, *rest):
    past_refs, (send_ref, amp_ref) = rest[:-2], rest[-2:]
    amp = amplitude_of(step, recv_ref, inc_ref, sinv_ref)
    amp_ref[...] = amp
    driven = (
        own_ref[step + 1]
        + a_ref[step].astype(F32)
        + b_ref[step].astype(F32)
        + c_ref[step].astype(F32)
    )
    for lag, past in enumerate([amp] + [r[...] for r in past_refs]):
        driven = driven + dot_f32(lag_ref[lag], past, ((0,), (0,)))
    field_of(driven, obs_ref, coup_ref, send_ref)


def last_kernel(recv_ref, inc_ref, sinv_ref, amp_ref):
    amp_ref[...] = amplitude_of(STEPS - 1, recv_ref, inc_ref, sinv_ref)


def call(kernel, name, outs, args):
    vmem = pl.BlockSpec(memory_space=pltpu.VMEM)
    return pl.pallas_call(
        kernel,
        name=name,
        out_shape=outs,
        in_specs=[vmem] * len(args),
        out_specs=jax.tree.map(lambda _: vmem, outs),
        compiler_params=pltpu.CompilerParams(vmem_limit_bytes=24 * 2**20),
    )(*args)


def on_device(history, interp_weights, pair_table, coupling, self_inverse, incident):
    patches, slab_len, src = history.shape
    pairs = pair_table.shape[1]
    local = coupling.shape[1]
    slabs = lax.axis_size("slab")
    blocks = lax.axis_size("patch")
    slab_id = lax.axis_index("slab")
    rows = patches * local

    def rolled(x):
        return lax.dynamic_slice_in_dim(jnp.concatenate([x, x], axis=1), slab_id * local, pairs, 1)

    table = rolled(pair_table)
    observer, first, band = table[..., 0], table[..., 1], table[..., 2]
    taps = jnp.arange(WMAX, dtype=jnp.int32)
    weights = jnp.where(taps < band[..., None], rolled(interp_weights).astype(F32), 0.0)
    steps = jnp.arange(STEPS, dtype=jnp.int32)
    start = first[:, None, :] - 1 - slab_id * slab_len - steps[:, None]
    start = start.reshape(patches, 1, STEPS * pairs).astype(F32)
    spread = jnp.tile(weights.transpose(0, 2, 1), (1, 1, STEPS))
    table_rows = jnp.concatenate([start, spread, jnp.zeros((patches, 3, STEPS * pairs), F32)], axis=1)
    obs = observer[:, :local].reshape(1, rows)
    lags = jnp.arange(1, STEPS, dtype=jnp.int32)
    hit = lags[:, None, None, None] - first[None, :, :local, None] == taps
    lag_w = jnp.sum(jnp.where(hit, weights[None, :, :local], 0.0), axis=-1)
    same = jnp.arange(patches)[:, None] == jnp.arange(rows)[None, :] // local
    lag_table = jnp.where(same[None], lag_w.reshape(LAGS, 1, rows), 0.0).astype(BF16)
    inc = incident.transpose(1, 0, 2)

    shape = jax.ShapeDtypeStruct
    outs = (
        [shape((STEPS, rows, src), F32)]
        + [shape((1, rows, src), BF16)] * (slabs - 1)
        + [shape((STEPS - 1, rows, src), BF16)] * (slabs - 1)
    )
    own, *sends = call(history_kernel, "history", outs, [table_rows, history])

    def moved(x, s):
        return lax.ppermute(x, "slab", [(z, (z + s) % slabs) for z in range(slabs)])

    now = [moved(x, s + 1) for s, x in enumerate(sends[: slabs - 1])]
    later = [moved(x, s + 1) for s, x in enumerate(sends[slabs - 1 :])]

    send_shape = shape((blocks, slabs, patches, src), BF16)
    send = call(first_kernel, "field0", send_shape, [own, *now, obs, coupling])
    amps = []
    for step in range(STEPS):
        recv = lax.all_to_all(
            send.reshape(blocks * slabs, patches, src), ("patch", "slab"), 0, 0, tiled=True
        )
        if step == STEPS - 1:
            amps.append(
                call(last_kernel, "last", shape((patches, src), BF16), [recv, inc, self_inverse])
            )
            break

        def body(*refs, step=step):
            step_kernel(step, *refs)

        send, amp = call(
            body,
            f"step{step}",
            [send_shape, shape((patches, src), BF16)],
            [recv, inc, self_inverse, lag_table, own, *later, obs, coupling, *amps[::-1]],
        )
        amps.append(amp)
    return jnp.stack(amps, axis=1)


def solution(mesh):
    in_specs = (
        P("patch", "slab", None),
        P("patch", None, None),
        P("patch", None, None),
        P("patch", "slab", None, None),
        P("patch", None, None),
        P("patch", None, None),
    )
    out_specs = P("patch", None, None)
    return jax.shard_map(
        on_device, mesh=mesh, in_specs=in_specs, out_specs=out_specs, check_vma=False
    )
```

```python
import jax
import jax.numpy as jnp
from jax import lax
from jax.experimental import pallas as pl
from jax.experimental.pallas import tpu as pltpu
from jax.sharding import PartitionSpec as P

WMAX = 4
STEPS = 4
LAGS = STEPS - 1

BF16 = jnp.bfloat16
F32 = jnp.float32


def dot_f32(a, b, contract):
    return lax.dot_general(a, b, (contract, ((), ())), preferred_element_type=F32)


def spread(values, group, keep):
    out = jnp.where(keep, values, 0.0)
    lanes = out.shape[1]
    step = group
    while step < lanes:
        out = out + pltpu.roll(out, step, 1)
        step *= 2
    return out


def tapped(at, weights):
    found = jnp.where(at == 0, weights[0], 0.0)
    for tap in range(1, WMAX):
        found = jnp.where(at == tap, weights[tap], found)
    return found


def history_kernel(table_hbm, weight_hbm, hist_hbm, own_ref, *rest):
    send_refs, (table_ref, weight_ref, hist_ref, sems) = rest[:-4], rest[-4:]
    copies = [
        pltpu.make_async_copy(src, dst, sems.at[i])
        for i, (src, dst) in enumerate(
            [(table_hbm, table_ref), (weight_hbm, weight_ref), (hist_hbm, hist_ref)]
        )
    ]
    for copy in copies:
        copy.start()
    patches, pairs = table_ref.shape[1:]
    _, slab_len, src = hist_ref.shape
    slabs = len(send_refs) + 1
    local = pairs // slabs
    slab_id = lax.axis_index("slab")
    lane = lax.broadcasted_iota(jnp.int32, (patches, src), 1)
    turn = lax.rem(src - slab_id * local, src)

    def widen(x):
        return pltpu.roll(jnp.concatenate([x.astype(F32)] * STEPS, axis=1), turn, 1)

    copies[0].wait()
    copies[1].wait()
    first, band = widen(table_ref[1]), widen(table_ref[2])
    wide = weight_ref[...].astype(F32)
    weights = [jnp.where(band > tap, widen(wide[:, tap, :]), 0.0) for tap in range(WMAX)]
    start = first - (lane // pairs + 1 + slab_id * slab_len).astype(F32)
    h = lax.broadcasted_iota(jnp.int32, (slab_len, src), 0).astype(F32)
    copies[2].wait()
    for p in range(0, patches, 2):
        parts = []
        for q in (p, p + 1):
            table = tapped(h - start[q : q + 1], [w[q : q + 1] for w in weights])
            parts.append(dot_f32(table.astype(BF16), hist_ref[q], ((0,), (0,))))
        at = pl.ds(p * local, 2 * local)
        for n in range(STEPS):
            for s in range(slabs):
                lo = n * pairs + s * local
                both = jnp.concatenate([part[lo : lo + local] for part in parts], axis=0)
                if s == 0:
                    own_ref[n, at, :] = both
                else:
                    send_refs[s - 1][n, at, :] = both.astype(BF16)


def prepare_kernel(table_ref, weight_ref, coup_ref, lag_ref, obs_ref, out_ref, sems):
    copies = [
        pltpu.make_async_copy(coup_ref.at[p], out_ref.at[p], sems.at[p])
        for p in range(coup_ref.shape[0])
    ]
    for copy in copies:
        copy.start()
    patches, pairs = table_ref.shape[1:]
    local, src = coup_ref.shape[1:3]
    slab_id = lax.axis_index("slab")
    core = lax.rem(lax.axis_index("patch"), 2)
    lane = lax.broadcasted_iota(jnp.int32, (patches, src), 1)
    row = lax.broadcasted_iota(jnp.int32, (patches, src), 0)
    mine = lane // local == slab_id
    blank = jnp.zeros((patches, src - pairs), F32)

    def widen(x):
        return spread(jnp.concatenate([x.astype(F32), blank], axis=1), local, mine)

    first, band = widen(table_ref[1]), widen(table_ref[2])
    obs = table_ref[0]
    obs = (obs // patches % 2 ^ core) * (patches * (lax.axis_size("patch") // 2)) + (
        obs // (2 * patches) * patches + obs % patches
    )
    diagonal = lane // local == row
    obs = jnp.sum(jnp.where(diagonal, widen(obs), 0.0), axis=0, keepdims=True)
    obs_ref[...] = jnp.broadcast_to(obs, obs_ref.shape).astype(jnp.int32)
    wide = weight_ref[...].astype(F32)
    weights = [jnp.where(band > tap, widen(wide[:, tap, :]), 0.0) for tap in range(WMAX)]
    lags = [jnp.where(diagonal, tapped(lag - first, weights), 0.0) for lag in range(1, STEPS)]
    lag_ref[...] = jnp.concatenate(lags, axis=0).astype(BF16)
    for copy in copies:
        copy.wait()


def field_of(driven, obs_ref, coup_ref, keep_ref, give_ref):
    rows, src = driven.shape
    patches = coup_ref.shape[0]
    local = rows // patches
    row_id = lax.broadcasted_iota(jnp.int32, (local, src), 0)
    coupled = []
    for p in range(patches):
        mine = driven[p * local : (p + 1) * local].astype(BF16)
        full = dot_f32(mine, coup_ref[p].reshape(local * src, src), ((1,), (1,)))
        out = full[:, :src]
        for k in range(1, local):
            out = jnp.where(row_id == k, full[:, k * src : (k + 1) * src], out)
        coupled.append(out)
    coupled = jnp.concatenate(coupled, axis=0).astype(BF16)
    half = keep_ref.shape[0]
    targets = lax.broadcasted_iota(jnp.int32, (2 * half, rows), 0)
    onehot = jnp.where(targets == obs_ref[0:1, :], 1.0, 0.0).astype(BF16)
    field = dot_f32(onehot, coupled, ((1,), (0,)))
    keep_ref[...] = field[:half]
    give_ref[...] = field[half:].astype(BF16)


def first_kernel(own_ref, a_ref, b_ref, c_ref, obs_ref, coup_ref, keep_ref, give_ref):
    driven = own_ref[0] + a_ref[0].astype(F32) + b_ref[0].astype(F32) + c_ref[0].astype(F32)
    field_of(driven, obs_ref, coup_ref, keep_ref, give_ref)


def join_kernel(keep_ref, got_ref, send_ref):
    blocks, slabs, patches, src = send_ref.shape
    total = (keep_ref[...] + got_ref[...].astype(F32)).astype(BF16).reshape(blocks, patches, src)
    for s in range(slabs):
        send_ref[:, s] = total


def amplitude_of(step, recv_ref, inc_ref, sinv_ref):
    sources, patches, src = recv_ref.shape
    total = jnp.sum(recv_ref[...].astype(F32), axis=0)
    drive = (inc_ref[:, step, :] - total).astype(BF16)
    row_id = lax.broadcasted_iota(jnp.int32, (patches, src), 0)
    amp = jnp.zeros((patches, src), F32)
    full = dot_f32(drive, sinv_ref[...].reshape(patches * src, src), ((1,), (1,)))
    for p in range(patches):
        amp = jnp.where(row_id == p, full[:, p * src : (p + 1) * src], amp)
    return amp.astype(BF16)


def step_kernel(step, recv_ref, inc_ref, sinv_ref, lag_ref, own_ref, a_ref, b_ref, c_ref, obs_ref, coup_ref, *rest):
    past_refs, (keep_ref, give_ref, amp_ref) = rest[:-3], rest[-3:]
    amp = amplitude_of(step, recv_ref, inc_ref, sinv_ref)
    amp_ref[...] = amp
    past = jnp.concatenate([amp] + [r[...] for r in past_refs], axis=0)
    driven = (
        own_ref[step + 1]
        + a_ref[step + 1].astype(F32)
        + b_ref[step + 1].astype(F32)
        + c_ref[step + 1].astype(F32)
        + dot_f32(lag_ref[: past.shape[0], :], past, ((0,), (0,)))
    )
    field_of(driven, obs_ref, coup_ref, keep_ref, give_ref)


def last_kernel(recv_ref, inc_ref, sinv_ref, *rest):
    past_refs, out_ref = rest[:-1], rest[-1]
    amp = amplitude_of(STEPS - 1, recv_ref, inc_ref, sinv_ref)
    for step, value in enumerate([r[...] for r in past_refs] + [amp]):
        out_ref[:, step, :] = value


def call(kernel, name, outs, args, spaces=None, scratch=(), cost=None):
    vmem = pl.BlockSpec(memory_space=pltpu.VMEM)
    spaces = spaces or [pltpu.VMEM] * len(args)
    return pl.pallas_call(
        kernel,
        name=name,
        out_shape=outs,
        in_specs=[pl.BlockSpec(memory_space=space) for space in spaces],
        out_specs=jax.tree.map(lambda _: vmem, outs),
        scratch_shapes=scratch,
        cost_estimate=cost,
        compiler_params=pltpu.CompilerParams(vmem_limit_bytes=24 * 2**20),
    )(*args)


def on_device(history, interp_weights, pair_table, coupling, self_inverse, incident):
    patches, slab_len, src = history.shape
    local = coupling.shape[1]
    slabs = lax.axis_size("slab")
    blocks = lax.axis_size("patch") // 2
    rows = patches * local
    half = blocks * patches
    cores = [(i, i ^ 1) for i in range(2 * blocks)]
    groups = [
        [(2 * b + core) * slabs + z for b in range(blocks) for z in range(slabs)] for core in range(2)
    ]

    def exchange(keep, give):
        got = lax.ppermute(give, "patch", cores)
        send = call(join_kernel, "join", shape((blocks, slabs, patches, src), BF16), [keep, got])
        send = send.reshape(blocks * slabs, patches, src)
        return lax.all_to_all(
            send, ("patch", "slab"), 0, 0, axis_index_groups=groups, tiled=True
        )

    shape = jax.ShapeDtypeStruct
    field = [shape((half, src), F32), shape((half, src), BF16)]
    table = pair_table.transpose(2, 0, 1)
    weight = interp_weights.transpose(0, 2, 1)
    own, *sends = call(
        history_kernel,
        "history",
        [shape((STEPS, rows, src), F32)] + [shape((STEPS, rows, src), BF16)] * (slabs - 1),
        [table, weight, history],
        spaces=[pltpu.HBM] * 3,
        scratch=[
            pltpu.VMEM(table.shape, jnp.int32),
            pltpu.VMEM(weight.shape, BF16),
            pltpu.VMEM(history.shape, BF16),
            pltpu.SemaphoreType.DMA((3,)),
        ],
    )
    parts = [
        lax.ppermute(x, "slab", [(z, (z + s + 1) % slabs) for z in range(slabs)])
        for s, x in enumerate(sends)
    ]
    lag_table, obs, near = call(
        prepare_kernel,
        "prepare",
        [
            shape((LAGS * patches, rows), BF16),
            shape((8, rows), jnp.int32),
            shape(coupling.shape, BF16),
        ],
        [table, weight, coupling],
        spaces=[pltpu.VMEM, pltpu.VMEM, pltpu.HBM],
        scratch=[pltpu.SemaphoreType.DMA((patches,))],
        cost=pl.CostEstimate(flops=0, bytes_accessed=4 * coupling.size, transcendentals=0),
    )
    keep, give = call(first_kernel, "first", field, [own, *parts, obs, near])
    amps = []
    for step in range(STEPS):
        recv = exchange(keep, give)
        if step == STEPS - 1:
            return call(
                last_kernel,
                "last",
                shape((patches, STEPS, src), BF16),
                [recv, incident, self_inverse, *amps],
            )

        def body(*refs, step=step):
            step_kernel(step, *refs)

        keep, give, amp = call(
            body,
            f"step{step}",
            field + [shape((patches, src), BF16)],
            [recv, incident, self_inverse, lag_table, own, *parts, obs, coupling, *amps[::-1]],
        )
        amps.append(amp)


def solution(mesh):
    in_specs = (
        P("patch", "slab", None),
        P("patch", None, None),
        P("patch", None, None),
        P("patch", "slab", None, None),
        P("patch", None, None),
        P("patch", None, None),
    )
    out_specs = P("patch", None, None)
    return jax.shard_map(
        on_device, mesh=mesh, in_specs=in_specs, out_specs=out_specs, check_vma=False
    )
```

```python
import functools

import jax
import jax.numpy as jnp
from jax import lax
from jax.experimental import pallas as pl
from jax.experimental.pallas import tpu as pltpu
from jax.sharding import PartitionSpec as P

WMAX = 4
STEPS = 4
LAGS = STEPS - 1

BF16 = jnp.bfloat16
F32 = jnp.float32


def dot_f32(a, b, contract):
    return lax.dot_general(a, b, (contract, ((), ())), preferred_element_type=F32)


def spread(values, group, keep):
    out = jnp.where(keep, values, 0.0)
    lanes = out.shape[1]
    step = group
    while step < lanes:
        out = out + pltpu.roll(out, step, 1)
        step *= 2
    return out


def tapped(at, weights):
    found = jnp.where(at == 0, weights[0], 0.0)
    for tap in range(1, WMAX):
        found = jnp.where(at == tap, weights[tap], found)
    return found


def start_copies(pairs, sems):
    copies = [pltpu.make_async_copy(src, dst, sems.at[i]) for i, (src, dst) in enumerate(pairs)]
    for copy in copies:
        copy.start()
    return copies


def history_kernel(table_hbm, weight_hbm, hist_hbm, own_ref, *rest):
    send_refs, (table_ref, weight_ref, hist_ref, sems) = rest[:-4], rest[-4:]
    copies = start_copies(
        [(table_hbm, table_ref), (weight_hbm, weight_ref), (hist_hbm, hist_ref)], sems
    )
    patches, pairs = table_ref.shape[1:]
    _, slab_len, src = hist_ref.shape
    slabs = len(send_refs) + 1
    local = pairs // slabs
    slab_id = lax.axis_index("slab")
    lane = lax.broadcasted_iota(jnp.int32, (patches, src), 1)
    turn = lax.rem(src - slab_id * local, src)

    def widen(x):
        return pltpu.roll(jnp.concatenate([x.astype(F32)] * STEPS, axis=1), turn, 1)

    copies[0].wait()
    copies[1].wait()
    first, band = widen(table_ref[1]), widen(table_ref[2])
    wide = weight_ref[...].astype(F32)
    weights = [jnp.where(band > tap, widen(wide[:, tap, :]), 0.0) for tap in range(WMAX)]
    start = first - (lane // pairs + 1 + slab_id * slab_len).astype(F32)
    h = lax.broadcasted_iota(jnp.int32, (slab_len, src), 0).astype(F32)
    copies[2].wait()
    for p in range(0, patches, 2):
        parts = []
        for q in (p, p + 1):
            table = tapped(h - start[q : q + 1], [w[q : q + 1] for w in weights])
            parts.append(dot_f32(table.astype(BF16), hist_ref[q], ((0,), (0,))))
        at = pl.ds(p * local, 2 * local)
        for n in range(STEPS):
            for s in range(slabs):
                lo = n * pairs + s * local
                both = jnp.concatenate([part[lo : lo + local] for part in parts], axis=0)
                if s == 0:
                    own_ref[n, at, :] = both
                else:
                    send_refs[s - 1][n, at, :] = both.astype(BF16)


def prepare_kernel(
    table_hbm, weight_hbm, coup_ref, lag_ref, obs_ref, out_ref, table_ref, weight_ref, sems
):
    copies = start_copies(
        [(table_hbm, table_ref), (weight_hbm, weight_ref)]
        + [(coup_ref.at[p], out_ref.at[p]) for p in range(coup_ref.shape[0])],
        sems,
    )
    copies[0].wait()
    copies[1].wait()
    patches, pairs = table_ref.shape[1:]
    local, src = coup_ref.shape[1:3]
    slab_id = lax.axis_index("slab")
    core = lax.rem(lax.axis_index("patch"), 2)
    lane = lax.broadcasted_iota(jnp.int32, (patches, src), 1)
    row = lax.broadcasted_iota(jnp.int32, (patches, src), 0)
    mine = lane // local == slab_id
    blank = jnp.zeros((patches, src - pairs), F32)

    def widen(x):
        return spread(jnp.concatenate([x.astype(F32), blank], axis=1), local, mine)

    first, band = widen(table_ref[1]), widen(table_ref[2])
    obs = table_ref[0]
    obs = (obs // patches % 2 ^ core) * (patches * (lax.axis_size("patch") // 2)) + (
        obs // (2 * patches) * patches + obs % patches
    )
    diagonal = lane // local == row
    obs = jnp.sum(jnp.where(diagonal, widen(obs), 0.0), axis=0, keepdims=True)
    obs_ref[...] = jnp.broadcast_to(obs, obs_ref.shape).astype(jnp.int32)
    wide = weight_ref[...].astype(F32)
    weights = [jnp.where(band > tap, widen(wide[:, tap, :]), 0.0) for tap in range(WMAX)]
    lags = [jnp.where(diagonal, tapped(lag - first, weights), 0.0) for lag in range(1, STEPS)]
    lag_ref[...] = jnp.concatenate(lags, axis=0).astype(BF16)
    for copy in copies[2:]:
        copy.wait()


def field_of(driven, obs_ref, coup_ref, keep_ref, give_ref):
    rows, src = driven.shape
    patches = coup_ref.shape[0]
    local = rows // patches
    row_id = lax.broadcasted_iota(jnp.int32, (local, src), 0)
    coupled = []
    for p in range(patches):
        mine = driven[p * local : (p + 1) * local].astype(BF16)
        full = dot_f32(mine, coup_ref[p].reshape(local * src, src), ((1,), (1,)))
        out = full[:, :src]
        for k in range(1, local):
            out = jnp.where(row_id == k, full[:, k * src : (k + 1) * src], out)
        coupled.append(out)
    coupled = jnp.concatenate(coupled, axis=0).astype(BF16)
    half = keep_ref.shape[0]
    targets = lax.broadcasted_iota(jnp.int32, (2 * half, rows), 0)
    onehot = jnp.where(targets == obs_ref[0:1, :], 1.0, 0.0).astype(BF16)
    field = dot_f32(onehot, coupled, ((1,), (0,)))
    keep_ref[...] = field[:half]
    give_ref[...] = field[half:].astype(BF16)


def first_kernel(own_ref, a_ref, b_ref, c_ref, obs_ref, coup_ref, keep_ref, give_ref):
    driven = own_ref[0] + a_ref[0].astype(F32) + b_ref[0].astype(F32) + c_ref[0].astype(F32)
    field_of(driven, obs_ref, coup_ref, keep_ref, give_ref)


def join_kernel(orders, keep_ref, got_ref, send_ref, total_ref):
    total = (keep_ref[...] + got_ref[...].astype(F32)).astype(BF16)
    total_ref[...] = total.reshape(total_ref.shape)
    core = lax.rem(lax.axis_index("patch"), 2)
    for i, (even, odd) in enumerate(zip(*orders)):
        send_ref[i] = total_ref[jnp.where(core == 0, even, odd)]


def amplitude_of(step, recv_ref, inc_ref, sinv_ref):
    sources, patches, src = recv_ref.shape
    total = jnp.sum(recv_ref[...].astype(F32), axis=0)
    drive = (inc_ref[:, step, :] - total).astype(BF16)
    row_id = lax.broadcasted_iota(jnp.int32, (patches, src), 0)
    amp = jnp.zeros((patches, src), F32)
    full = dot_f32(drive, sinv_ref[...].reshape(patches * src, src), ((1,), (1,)))
    for p in range(patches):
        amp = jnp.where(row_id == p, full[:, p * src : (p + 1) * src], amp)
    return amp.astype(BF16)


def step_kernel(step, recv_ref, inc_ref, sinv_ref, lag_ref, own_ref, a_ref, b_ref, c_ref, obs_ref, coup_ref, *rest):
    past_refs, (keep_ref, give_ref, amp_ref) = rest[:-3], rest[-3:]
    amp = amplitude_of(step, recv_ref, inc_ref, sinv_ref)
    amp_ref[...] = amp
    past = jnp.concatenate([amp] + [r[...] for r in past_refs], axis=0)
    driven = (
        own_ref[step + 1]
        + a_ref[step + 1].astype(F32)
        + b_ref[step + 1].astype(F32)
        + c_ref[step + 1].astype(F32)
        + dot_f32(lag_ref[: past.shape[0], :], past, ((0,), (0,)))
    )
    field_of(driven, obs_ref, coup_ref, keep_ref, give_ref)


def last_kernel(recv_ref, inc_ref, sinv_ref, *rest):
    past_refs, out_ref = rest[:-1], rest[-1]
    amp = amplitude_of(STEPS - 1, recv_ref, inc_ref, sinv_ref)
    for step, value in enumerate([r[...] for r in past_refs] + [amp]):
        out_ref[:, step, :] = value


def call(kernel, name, outs, args, in_hbm=False, scratch=(), cost=None):
    vmem = pl.BlockSpec(memory_space=pltpu.VMEM)
    space = pltpu.HBM if in_hbm else pltpu.VMEM
    if in_hbm:
        args = [pltpu.with_memory_space_constraint(x, pltpu.HBM) for x in args]
    return pl.pallas_call(
        kernel,
        name=name,
        out_shape=outs,
        in_specs=[pl.BlockSpec(memory_space=space)] * len(args),
        out_specs=jax.tree.map(lambda _: vmem, outs),
        scratch_shapes=scratch,
        cost_estimate=cost,
        compiler_params=pltpu.CompilerParams(vmem_limit_bytes=24 * 2**20),
    )(*args)


def around(n):
    return [i ^ (i >> 1) for i in range(n)]


def on_device(history, interp_weights, pair_table, coupling, self_inverse, incident):
    patches, slab_len, src = history.shape
    local = coupling.shape[1]
    slabs = lax.axis_size("slab")
    blocks = lax.axis_size("patch") // 2
    rows = patches * local
    half = blocks * patches
    cores = [(i, i ^ 1) for i in range(2 * blocks)]
    wide = next(n for n in range(1, blocks + 1) if n * n >= blocks)
    chips = [
        [(y * wide + x, z) for y in around(blocks // wide) for x in around(wide) for z in around(slabs)],
        [(y * wide + x, z) for x in around(wide) for z in around(slabs) for y in around(blocks // wide)],
    ]
    groups = [[(2 * b + core) * slabs + z for b, z in chips[core]] for core in range(2)]
    orders = [[b for b, _ in chips[core]] for core in range(2)]

    def exchange(keep, give):
        got = lax.ppermute(give, "patch", cores)
        send = call(
            functools.partial(join_kernel, orders),
            "join",
            shape((blocks * slabs, patches, src), BF16),
            [keep, got],
            scratch=[pltpu.VMEM((blocks, patches, src), BF16)],
        )
        return lax.all_to_all(
            send, ("patch", "slab"), 0, 0, axis_index_groups=groups, tiled=True
        )

    shape = jax.ShapeDtypeStruct
    field = [shape((half, src), F32), shape((half, src), BF16)]
    table = pair_table.transpose(2, 0, 1)
    weight = interp_weights.transpose(0, 2, 1)
    own, *sends = call(
        history_kernel,
        "history",
        [shape((STEPS, rows, src), F32)] + [shape((STEPS, rows, src), BF16)] * (slabs - 1),
        [table, weight, history],
        in_hbm=True,
        scratch=[
            pltpu.VMEM(table.shape, jnp.int32),
            pltpu.VMEM(weight.shape, BF16),
            pltpu.VMEM(history.shape, BF16),
            pltpu.SemaphoreType.DMA((3,)),
        ],
    )
    parts = [
        lax.ppermute(x, "slab", [(z, (z + s + 1) % slabs) for z in range(slabs)])
        for s, x in enumerate(sends)
    ]
    lag_table, obs, near = call(
        prepare_kernel,
        "prepare",
        [
            shape((LAGS * patches, rows), BF16),
            shape((8, rows), jnp.int32),
            shape(coupling.shape, BF16),
        ],
        [table, weight, coupling],
        in_hbm=True,
        scratch=[
            pltpu.VMEM(table.shape, jnp.int32),
            pltpu.VMEM(weight.shape, BF16),
            pltpu.SemaphoreType.DMA((2 + patches,)),
        ],
        cost=pl.CostEstimate(flops=0, bytes_accessed=4 * coupling.size, transcendentals=0),
    )
    keep, give = call(first_kernel, "first", field, [own, *parts, obs, near])
    amps = []
    for step in range(STEPS):
        recv = exchange(keep, give)
        if step == STEPS - 1:
            return call(
                last_kernel,
                "last",
                shape((patches, STEPS, src), BF16),
                [recv, incident, self_inverse, *amps],
            )

        def body(*refs, step=step):
            step_kernel(step, *refs)

        keep, give, amp = call(
            body,
            f"step{step}",
            field + [shape((patches, src), BF16)],
            [recv, incident, self_inverse, lag_table, own, *parts, obs, coupling, *amps[::-1]],
        )
        amps.append(amp)


def solution(mesh):
    in_specs = (
        P("patch", "slab", None),
        P("patch", None, None),
        P("patch", None, None),
        P("patch", "slab", None, None),
        P("patch", None, None),
        P("patch", None, None),
    )
    out_specs = P("patch", None, None)
    return jax.shard_map(
        on_device, mesh=mesh, in_specs=in_specs, out_specs=out_specs, check_vma=False
    )
```

```python
import functools
import math

import jax
import jax.numpy as jnp
from jax import lax
from jax.experimental import pallas as pl
from jax.experimental.pallas import tpu as pltpu
from jax.sharding import PartitionSpec as P

WMAX = 4
STEPS = 4
LAGS = STEPS - 1
STRIDE = 37

BF16 = jnp.bfloat16
F32 = jnp.float32


def dot_f32(a, b, contract):
    return lax.dot_general(a, b, (contract, ((), ())), preferred_element_type=F32)


def spread(values, group, keep):
    out = jnp.where(keep, values, 0.0)
    lanes = out.shape[1]
    step = group
    while step < lanes:
        out = out + pltpu.roll(out, step, 1)
        step *= 2
    return out


def tapped(at, weights):
    found = jnp.where(at == 0, weights[0], 0.0)
    for tap in range(1, WMAX):
        found = jnp.where(at == tap, weights[tap], found)
    return found


def start_copies(pairs, sems):
    copies = [pltpu.make_async_copy(src, dst, sems.at[i]) for i, (src, dst) in enumerate(pairs)]
    for copy in copies:
        copy.start()
    return copies


def history_kernel(plan, table_hbm, weight_hbm, hist_hbm, own_ref, *rest):
    send_refs, (table_ref, weight_ref, hist_ref, sems) = rest[:-4], rest[-4:]
    copies = start_copies(
        [(table_hbm, table_ref), (weight_hbm, weight_ref), (hist_hbm, hist_ref)], sems
    )
    patches, pairs = table_ref.shape[1:]
    _, slab_len, src = hist_ref.shape
    local = own_ref.shape[1] // patches
    slab_id = lax.axis_index("slab")
    lane = lax.broadcasted_iota(jnp.int32, (patches, src), 1)
    turn = lax.rem(src - slab_id * local, src)

    def widen(x):
        return pltpu.roll(jnp.concatenate([x.astype(F32)] * STEPS, axis=1), turn, 1)

    copies[0].wait()
    copies[1].wait()
    first, band = widen(table_ref[1]), widen(table_ref[2])
    wide = weight_ref[...].astype(F32)
    weights = [jnp.where(band > tap, widen(wide[:, tap, :]), 0.0) for tap in range(WMAX)]
    start = first - (lane // pairs + 1 + slab_id * slab_len).astype(F32)

    h = lax.broadcasted_iota(jnp.int32, (slab_len, src), 0).astype(F32)
    copies[2].wait()
    for p in range(0, patches, 2):
        parts = []
        for q in (p, p + 1):
            table = tapped(h - start[q : q + 1], [w[q : q + 1] for w in weights])
            parts.append(dot_f32(table.astype(BF16), hist_ref[q], ((0,), (0,))))
        at = pl.ds(p * local, 2 * local)
        for n in range(STEPS):
            for (s, steps), out_ref in zip(((0, range(STEPS)),) + plan, (own_ref,) + send_refs):
                if n in steps:
                    lo = n * pairs + s * local
                    both = jnp.concatenate([part[lo : lo + local] for part in parts], axis=0)
                    out_ref[n - steps[0], at, :] = both.astype(out_ref.dtype)


def tables_kernel(local, table_hbm, weight_hbm, lag_ref, onehot_ref, table_ref, weight_ref, sems):
    copies = start_copies([(table_hbm, table_ref), (weight_hbm, weight_ref)], sems)
    patches, pairs = table_ref.shape[1:]
    rows = onehot_ref.shape[1]
    slab_id = lax.axis_index("slab")
    core = lax.rem(lax.axis_index("patch"), 2)
    lane = lax.broadcasted_iota(jnp.int32, (patches, rows), 1)
    row = lax.broadcasted_iota(jnp.int32, (patches, rows), 0)
    mine = lane // local == slab_id
    diagonal = lane // local == row
    blank = jnp.zeros((patches, rows - pairs), F32)

    def widen(x):
        return spread(jnp.concatenate([x.astype(F32), blank], axis=1), local, mine)

    for copy in copies:
        copy.wait()
    first, band = widen(table_ref[1]), widen(table_ref[2])
    wide = weight_ref[...].astype(F32)
    weights = [jnp.where(band > tap, widen(wide[:, tap, :]), 0.0) for tap in range(WMAX)]
    lags = [jnp.where(diagonal, tapped(lag - first, weights), 0.0) for lag in range(1, STEPS)]
    lag_ref[...] = jnp.concatenate(lags, axis=0).astype(BF16)
    obs = table_ref[0]
    obs = (obs // patches % 2 ^ core) * (patches * (lax.axis_size("patch") // 2)) + (
        obs // (2 * patches) * patches + obs % patches
    )
    obs = jnp.sum(jnp.where(diagonal, widen(obs), 0.0), axis=0, keepdims=True).astype(jnp.int32)
    targets = lax.broadcasted_iota(jnp.int32, onehot_ref.shape, 0)
    onehot_ref[...] = jnp.where(targets == obs, 1.0, 0.0).astype(BF16)


def field_of(driven, onehot_ref, coup_ref, coupled_ref, give_ref):
    rows, src = driven.shape
    patches = coup_ref.shape[0]
    local = rows // patches
    row_id = lax.broadcasted_iota(jnp.int32, (local, src), 0)
    coupled = []
    for p in range(patches):
        mine = driven[p * local : (p + 1) * local].astype(BF16)
        full = dot_f32(mine, coup_ref[p].reshape(local * src, src), ((1,), (1,)))
        out = full[:, :src]
        for k in range(1, local):
            out = jnp.where(row_id == k, full[:, k * src : (k + 1) * src], out)
        coupled.append(out)
    coupled = jnp.concatenate(coupled, axis=0).astype(BF16)
    coupled_ref[...] = coupled
    give_ref[...] = dot_f32(onehot_ref[give_ref.shape[0] :], coupled, ((1,), (0,))).astype(BF16)


def keep_kernel(onehot_ref, coupled_ref, keep_ref):
    keep_ref[...] = dot_f32(onehot_ref[: keep_ref.shape[0]], coupled_ref[...], ((1,), (0,)))


def first_kernel(own_ref, *rest):
    part_refs, tail = rest[:-4], rest[-4:]
    driven = own_ref[0]
    for part in part_refs:
        driven = driven + part[0].astype(F32)
    field_of(driven, *tail)


def add_kernel(orders, plan, keep_ref, got_ref, own_ref, *rest):
    part_refs, (send_ref, stored_ref, total_ref) = rest[:-3], rest[-3:]
    join_kernel(orders, keep_ref, got_ref, send_ref, total_ref)
    for n in range(1, STEPS):
        stored = own_ref[n]
        for (_, steps), part in zip(plan, part_refs):
            if n in steps:
                stored = stored + part[n - steps[0]].astype(F32)
        stored_ref[n - 1] = stored


def join_kernel(orders, keep_ref, got_ref, send_ref, total_ref):
    total = (keep_ref[...] + got_ref[...].astype(F32)).astype(BF16)
    total_ref[...] = total.reshape(total_ref.shape)
    core = lax.rem(lax.axis_index("patch"), 2)
    for which, order in enumerate(orders):

        @pl.when(core == which)
        def _(order=order):
            for i, block in enumerate(order):
                send_ref[i] = total_ref[block]


def amplitude_of(step, recv_ref, inc_ref, sinv_ref):
    sources, patches, src = recv_ref.shape
    total = jnp.sum(recv_ref[...].astype(F32), axis=0)
    drive = (inc_ref[:, step, :] - total).astype(BF16)
    row_id = lax.broadcasted_iota(jnp.int32, (patches, src), 0)
    amp = jnp.zeros((patches, src), F32)
    full = dot_f32(drive, sinv_ref[...].reshape(patches * src, src), ((1,), (1,)))
    for p in range(patches):
        amp = jnp.where(row_id == p, full[:, p * src : (p + 1) * src], amp)
    return amp.astype(BF16)


def step_kernel(step, recv_ref, inc_ref, sinv_ref, lag_ref, stored_ref, onehot_ref, coup_ref, *rest):
    past_refs, (coupled_ref, give_ref, amp_ref) = rest[:-3], rest[-3:]
    amp = amplitude_of(step, recv_ref, inc_ref, sinv_ref)
    amp_ref[...] = amp
    past = jnp.concatenate([amp] + [r[...] for r in past_refs], axis=0)
    driven = stored_ref[step] + dot_f32(lag_ref[: past.shape[0], :], past, ((0,), (0,)))
    field_of(driven, onehot_ref, coup_ref, coupled_ref, give_ref)


def last_kernel(recv_ref, inc_ref, sinv_ref, *rest):
    past_refs, out_ref = rest[:-1], rest[-1]
    amp = amplitude_of(STEPS - 1, recv_ref, inc_ref, sinv_ref)
    for step, value in enumerate([r[...] for r in past_refs] + [amp]):
        out_ref[:, step, :] = value


def call(kernel, name, outs, args, in_hbm=False, scratch=(), cost=None):
    vmem = pl.BlockSpec(memory_space=pltpu.VMEM)
    space = pltpu.HBM if in_hbm else pltpu.VMEM
    if in_hbm:
        args = [pltpu.with_memory_space_constraint(x, pltpu.HBM) for x in args]
    return pl.pallas_call(
        kernel,
        name=name,
        out_shape=outs,
        in_specs=[pl.BlockSpec(memory_space=space)] * len(args),
        out_specs=jax.tree.map(lambda _: vmem, outs),
        scratch_shapes=scratch,
        cost_estimate=cost,
        compiler_params=pltpu.CompilerParams(vmem_limit_bytes=24 * 2**20),
    )(*args)


def around(n):
    return [i ^ (i >> 1) for i in range(n)]


def on_device(history, interp_weights, pair_table, coupling, self_inverse, incident):
    patches, slab_len, src = history.shape
    local = coupling.shape[1]
    slabs = lax.axis_size("slab")
    blocks = lax.axis_size("patch") // 2
    rows = patches * local
    half = blocks * patches
    cores = [(i, i ^ 1) for i in range(2 * blocks)]
    wide = next(n for n in range(1, blocks + 1) if n * n >= blocks)
    chips = [
        [(y * wide + x, z) for y in around(blocks // wide) for x in around(wide) for z in around(slabs)],
        [(y * wide + x, z) for x in around(wide) for z in around(slabs) for y in around(blocks // wide)],
    ]
    count = len(chips[0])
    chips[0] = [chips[0][i * STRIDE % count] for i in range(count)] if math.gcd(STRIDE, count) == 1 else chips[0]
    groups = [[(2 * b + core) * slabs + z for b, z in chips[core]] for core in range(2)]
    orders = [[b for b, _ in chips[core]] for core in range(2)]

    def exchange(coupled, give, history=None):
        got = lax.ppermute(give, "patch", cores)
        keep = call(keep_kernel, "keep", shape((half, src), F32), [onehot, coupled])
        out = shape((blocks * slabs, patches, src), BF16)
        scratch = [pltpu.VMEM((blocks, patches, src), BF16)]
        if history:
            kernel = functools.partial(add_kernel, orders, plan)
            outs = [out, shape((STEPS - 1, rows, src), F32)]
            send, *stored = call(kernel, "add", outs, [keep, got, *history], scratch=scratch)
        else:
            kernel, stored = functools.partial(join_kernel, orders), []
            send = call(kernel, "join", out, [keep, got], scratch=scratch)
        recv = lax.all_to_all(send, ("patch", "slab"), 0, 0, axis_index_groups=groups, tiled=True)
        return recv, *stored

    shape = jax.ShapeDtypeStruct
    field = [shape((rows, src), BF16), shape((half, src), BF16)]
    table = pair_table.transpose(2, 0, 1)
    weight = interp_weights.transpose(0, 2, 1)
    far = slabs // 2
    order = [far] + [s for s in range(slabs - 1, 0, -1) if s != far]
    plan = tuple((s, range(STEPS)) for s in order)
    own, *sends = call(
        functools.partial(history_kernel, plan),
        "history",
        [
            shape((STEPS, rows, src), F32),
            *(shape((len(steps), rows, src), BF16) for _, steps in plan),
        ],
        [table, weight, history],
        in_hbm=True,
        scratch=[
            pltpu.VMEM(table.shape, jnp.int32),
            pltpu.VMEM(weight.shape, BF16),
            pltpu.VMEM(history.shape, BF16),
            pltpu.SemaphoreType.DMA((3,)),
        ],
        cost=pl.CostEstimate(flops=10**10, bytes_accessed=10**7, transcendentals=0),
    )
    parts = [
        lax.ppermute(x, "slab", [(z, (z + s) % slabs) for z in range(slabs)])
        for (s, _), x in zip(plan, sends)
    ]
    lag_table, onehot = call(
        functools.partial(tables_kernel, local),
        "tables",
        [shape((LAGS * patches, rows), BF16), shape((2 * half, rows), BF16)],
        [table, weight],
        in_hbm=True,
        scratch=[
            pltpu.VMEM(table.shape, jnp.int32),
            pltpu.VMEM(weight.shape, BF16),
            pltpu.SemaphoreType.DMA((2,)),
        ],
    )
    coupled, give = call(first_kernel, "first", field, [own, *parts, onehot, coupling])
    amps = []
    for step in range(STEPS):
        if step == 0:
            recv, stored = exchange(coupled, give, [own, *parts])
        else:
            (recv,) = exchange(coupled, give)
        if step == STEPS - 1:
            return call(
                last_kernel,
                "last",
                shape((patches, STEPS, src), BF16),
                [recv, incident, self_inverse, *amps],
            )

        def body(*refs, step=step):
            step_kernel(step, *refs)

        coupled, give, amp = call(
            body,
            f"step{step}",
            field + [shape((patches, src), BF16)],
            [recv, incident, self_inverse, lag_table, stored, onehot, coupling, *amps[::-1]],
        )
        amps.append(amp)


def solution(mesh):
    in_specs = (
        P("patch", "slab", None),
        P("patch", None, None),
        P("patch", None, None),
        P("patch", "slab", None, None),
        P("patch", None, None),
        P("patch", None, None),
    )
    out_specs = P("patch", None, None)
    return jax.shard_map(
        on_device, mesh=mesh, in_specs=in_specs, out_specs=out_specs, check_vma=False
    )
```

```python
import functools
import math

import jax
import jax.numpy as jnp
from jax import lax
from jax.experimental import pallas as pl
from jax.experimental.pallas import tpu as pltpu
from jax.sharding import PartitionSpec as P

WMAX = 4
STEPS = 4
LAGS = STEPS - 1
STRIDE = 37
TURNED = 2

BF16 = jnp.bfloat16
F32 = jnp.float32


def dot_f32(a, b, contract):
    return lax.dot_general(a, b, (contract, ((), ())), preferred_element_type=F32)


def spread(values, group, keep):
    out = jnp.where(keep, values, 0.0)
    lanes = out.shape[1]
    step = group
    while step < lanes:
        out = out + pltpu.roll(out, step, 1)
        step *= 2
    return out


def tapped(at, weights):
    found = jnp.where(at == 0, weights[0], 0.0)
    for tap in range(1, WMAX):
        found = jnp.where(at == tap, weights[tap], found)
    return found


def start_copies(pairs, sems):
    copies = [pltpu.make_async_copy(src, dst, sems.at[i]) for i, (src, dst) in enumerate(pairs)]
    for copy in copies:
        copy.start()
    return copies


def history_kernel(plan, table_hbm, weight_hbm, hist_hbm, own_ref, *rest):
    send_refs, (table_ref, weight_ref, hist_ref, sems) = rest[:-4], rest[-4:]
    copies = start_copies(
        [(table_hbm, table_ref), (weight_hbm, weight_ref), (hist_hbm, hist_ref)], sems
    )
    patches, pairs = table_ref.shape[1:]
    _, slab_len, src = hist_ref.shape
    local = own_ref.shape[1] // patches
    slab_id = lax.axis_index("slab")
    lane = lax.broadcasted_iota(jnp.int32, (patches, src), 1)
    turn = lax.rem(src - slab_id * local, src)

    def widen(x):
        return pltpu.roll(jnp.concatenate([x.astype(F32)] * STEPS, axis=1), turn, 1)

    copies[0].wait()
    copies[1].wait()
    first, band = widen(table_ref[1]), widen(table_ref[2])
    wide = weight_ref[...].astype(F32)
    weights = [jnp.where(band > tap, widen(wide[:, tap, :]), 0.0) for tap in range(WMAX)]
    start = first - (lane // pairs + 1 + slab_id * slab_len).astype(F32)

    h = lax.broadcasted_iota(jnp.int32, (slab_len, src), 0).astype(F32)
    copies[2].wait()
    for p in range(0, patches, 2):
        parts = []
        for q in (p, p + 1):
            table = tapped(h - start[q : q + 1], [w[q : q + 1] for w in weights])
            parts.append(dot_f32(table.astype(BF16), hist_ref[q], ((0,), (0,))))
        at = pl.ds(p * local, 2 * local)
        for n in range(STEPS):
            for (s, steps), out_ref in zip(((0, range(STEPS)),) + plan, (own_ref,) + send_refs):
                if n in steps:
                    lo = n * pairs + s * local
                    both = jnp.concatenate([part[lo : lo + local] for part in parts], axis=0)
                    out_ref[n - steps[0], at, :] = both.astype(out_ref.dtype)


def tables_kernel(local, table_hbm, weight_hbm, lag_ref, onehot_ref, table_ref, weight_ref, sems):
    copies = start_copies([(table_hbm, table_ref), (weight_hbm, weight_ref)], sems)
    patches, pairs = table_ref.shape[1:]
    rows = onehot_ref.shape[1]
    slab_id = lax.axis_index("slab")
    core = lax.rem(lax.axis_index("patch"), 2)
    lane = lax.broadcasted_iota(jnp.int32, (patches, rows), 1)
    row = lax.broadcasted_iota(jnp.int32, (patches, rows), 0)
    mine = lane // local == slab_id
    diagonal = lane // local == row
    blank = jnp.zeros((patches, rows - pairs), F32)

    def widen(x):
        return spread(jnp.concatenate([x.astype(F32), blank], axis=1), local, mine)

    for copy in copies:
        copy.wait()
    first, band = widen(table_ref[1]), widen(table_ref[2])
    wide = weight_ref[...].astype(F32)
    weights = [jnp.where(band > tap, widen(wide[:, tap, :]), 0.0) for tap in range(WMAX)]
    lags = [jnp.where(diagonal, tapped(lag - first, weights), 0.0) for lag in range(1, STEPS)]
    rest = jnp.zeros((rows - LAGS * patches, rows), F32)
    lag_ref[...] = jnp.concatenate(lags + [rest], axis=0).T.astype(BF16)
    obs = table_ref[0]
    obs = (obs // patches % 2 ^ core) * (patches * (lax.axis_size("patch") // 2)) + (
        obs // (2 * patches) * patches + obs % patches
    )
    obs = jnp.sum(jnp.where(diagonal, widen(obs), 0.0), axis=0, keepdims=True).astype(jnp.int32)
    targets = lax.broadcasted_iota(jnp.int32, onehot_ref.shape, 0)
    onehot_ref[...] = jnp.where(targets == obs, 1.0, 0.0).astype(BF16)


def turn_kernel(coup_ref, turned_ref):
    patches, count = turned_ref.shape[:2]
    skip = coup_ref.shape[1] - count
    for p in range(patches):
        for i in range(count):
            turned_ref[p, i] = coup_ref[p, skip + i].astype(F32).T.astype(BF16)


def field_of(driven, onehot_ref, coup_ref, turned_ref, coupled_ref, give_ref):
    rows, src = driven.shape
    patches, local = coup_ref.shape[:2]
    direct = local - turned_ref.shape[1]
    row_id = lax.broadcasted_iota(jnp.int32, (local, src), 0)
    driven = driven.astype(BF16).astype(F32)
    columns = driven.T
    coupled = []
    for p in range(patches):
        mine = driven[p * local : (p + 1) * local].astype(BF16)
        full = dot_f32(mine, coup_ref[p, :direct].reshape(direct * src, src), ((1,), (1,)))
        out = full[:, :src]
        for k in range(1, direct):
            out = jnp.where(row_id == k, full[:, k * src : (k + 1) * src], out)
        for k in range(direct, local):
            r = p * local + k
            terms = turned_ref[p, k - direct].astype(F32) * columns[:, r : r + 1]
            out = jnp.where(row_id == k, jnp.sum(terms, axis=0, keepdims=True), out)
        coupled.append(out)
    coupled = jnp.concatenate(coupled, axis=0).astype(BF16)
    coupled_ref[...] = coupled
    give_ref[...] = dot_f32(onehot_ref[give_ref.shape[0] :], coupled, ((1,), (0,))).astype(BF16)


def keep_kernel(onehot_ref, coupled_ref, keep_ref):
    keep_ref[...] = dot_f32(onehot_ref[: keep_ref.shape[0]], coupled_ref[...], ((1,), (0,)))


def first_kernel(own_ref, *rest):
    part_refs, tail = rest[:-5], rest[-5:]
    driven = own_ref[0]
    for part in part_refs:
        driven = driven + part[0].astype(F32)
    field_of(driven, *tail)


def add_kernel(orders, plan, keep_ref, got_ref, own_ref, *rest):
    part_refs, (send_ref, stored_ref, total_ref) = rest[:-3], rest[-3:]
    join_kernel(orders, keep_ref, got_ref, send_ref, total_ref)
    for n in range(1, STEPS):
        stored = own_ref[n]
        for (_, steps), part in zip(plan, part_refs):
            if n in steps:
                stored = stored + part[n - steps[0]].astype(F32)
        stored_ref[n - 1] = stored


def join_kernel(orders, keep_ref, got_ref, send_ref, total_ref):
    total = (keep_ref[...] + got_ref[...].astype(F32)).astype(BF16)
    total_ref[...] = total.reshape(total_ref.shape)
    core = lax.rem(lax.axis_index("patch"), 2)
    for which, order in enumerate(orders):

        @pl.when(core == which)
        def _(order=order):
            for i, block in enumerate(order):
                send_ref[i] = total_ref[block]


def amplitude_of(step, recv_ref, inc_ref, sinv_ref):
    sources, patches, src = recv_ref.shape
    total = jnp.sum(recv_ref[...].astype(F32), axis=0)
    drive = inc_ref[:, step, :] - total
    halves = []
    group = 8
    row_id = lax.broadcasted_iota(jnp.int32, (group, src), 0)
    for p in range(0, patches, group):
        matrices = sinv_ref[p : p + group].reshape(group * src, src)
        full = dot_f32(drive[p : p + group].astype(BF16), matrices, ((1,), (1,)))
        amp = full[:, :src]
        for i in range(1, group):
            amp = jnp.where(row_id == i, full[:, i * src : (i + 1) * src], amp)
        halves.append(amp)
    amp = jnp.concatenate(halves, axis=0)
    return amp.astype(BF16)


def step_kernel(step, recv_ref, inc_ref, sinv_ref, lag_ref, stored_ref, onehot_ref, coup_ref, turned_ref, *rest):
    past_refs, (coupled_ref, give_ref, amp_ref) = rest[:-3], rest[-3:]
    amp = amplitude_of(step, recv_ref, inc_ref, sinv_ref)
    amp_ref[...] = amp
    past = jnp.concatenate([amp] + [r[...] for r in past_refs], axis=0)
    driven = stored_ref[step] + dot_f32(lag_ref[:, : past.shape[0]], past, ((1,), (0,)))
    field_of(driven, onehot_ref, coup_ref, turned_ref, coupled_ref, give_ref)


def last_kernel(recv_ref, inc_ref, sinv_ref, *rest):
    past_refs, out_ref = rest[:-1], rest[-1]
    amp = amplitude_of(STEPS - 1, recv_ref, inc_ref, sinv_ref)
    for step, value in enumerate([r[...] for r in past_refs] + [amp]):
        out_ref[:, step, :] = value


def call(kernel, name, outs, args, in_hbm=False, scratch=(), cost=None):
    vmem = pl.BlockSpec(memory_space=pltpu.VMEM)
    space = pltpu.HBM if in_hbm else pltpu.VMEM
    if in_hbm:
        args = [pltpu.with_memory_space_constraint(x, pltpu.HBM) for x in args]
    return pl.pallas_call(
        kernel,
        name=name,
        out_shape=outs,
        in_specs=[pl.BlockSpec(memory_space=space)] * len(args),
        out_specs=jax.tree.map(lambda _: vmem, outs),
        scratch_shapes=scratch,
        cost_estimate=cost,
        compiler_params=pltpu.CompilerParams(vmem_limit_bytes=24 * 2**20),
    )(*args)


def around(n):
    return [i ^ (i >> 1) for i in range(n)]


def on_device(history, interp_weights, pair_table, coupling, self_inverse, incident):
    patches, slab_len, src = history.shape
    local = coupling.shape[1]
    slabs = lax.axis_size("slab")
    blocks = lax.axis_size("patch") // 2
    rows = patches * local
    half = blocks * patches
    cores = [(i, i ^ 1) for i in range(2 * blocks)]
    wide = next(n for n in range(1, blocks + 1) if n * n >= blocks)
    chips = [
        [(y * wide + x, z) for y in around(blocks // wide) for x in around(wide) for z in around(slabs)],
        [(y * wide + x, z) for x in around(wide) for z in around(slabs) for y in around(blocks // wide)],
    ]
    count = len(chips[0])
    chips[0] = [chips[0][i * STRIDE % count] for i in range(count)] if math.gcd(STRIDE, count) == 1 else chips[0]
    groups = [[(2 * b + core) * slabs + z for b, z in chips[core]] for core in range(2)]
    orders = [[b for b, _ in chips[core]] for core in range(2)]

    def exchange(coupled, give, history=None):
        got = lax.ppermute(give, "patch", cores)
        keep = call(keep_kernel, "keep", shape((half, src), F32), [onehot, coupled])
        out = shape((blocks * slabs, patches, src), BF16)
        scratch = [pltpu.VMEM((blocks, patches, src), BF16)]
        if history:
            kernel = functools.partial(add_kernel, orders, plan)
            outs = [out, shape((STEPS - 1, rows, src), F32)]
            send, *stored = call(kernel, "add", outs, [keep, got, *history], scratch=scratch)
        else:
            kernel, stored = functools.partial(join_kernel, orders), []
            send = call(kernel, "join", out, [keep, got], scratch=scratch)
        recv = lax.all_to_all(send, ("patch", "slab"), 0, 0, axis_index_groups=groups, tiled=True)
        return recv, *stored

    shape = jax.ShapeDtypeStruct
    field = [shape((rows, src), BF16), shape((half, src), BF16)]
    table = pair_table.transpose(2, 0, 1)
    weight = interp_weights.transpose(0, 2, 1)
    far = slabs // 2
    order = [far] + [s for s in range(slabs - 1, 0, -1) if s != far]
    plan = tuple((s, range(STEPS)) for s in order)
    own, *sends = call(
        functools.partial(history_kernel, plan),
        "history",
        [
            shape((STEPS, rows, src), F32),
            *(shape((len(steps), rows, src), BF16) for _, steps in plan),
        ],
        [table, weight, history],
        in_hbm=True,
        scratch=[
            pltpu.VMEM(table.shape, jnp.int32),
            pltpu.VMEM(weight.shape, BF16),
            pltpu.VMEM(history.shape, BF16),
            pltpu.SemaphoreType.DMA((3,)),
        ],
        cost=pl.CostEstimate(flops=10**10, bytes_accessed=10**7, transcendentals=0),
    )
    parts = [
        lax.ppermute(x, "slab", [(z, (z + s) % slabs) for z in range(slabs)])
        for (s, _), x in zip(plan, sends)
    ]
    lag_table, onehot = call(
        functools.partial(tables_kernel, local),
        "tables",
        [shape((rows, rows), BF16), shape((2 * half, rows), BF16)],
        [table, weight],
        in_hbm=True,
        scratch=[
            pltpu.VMEM(table.shape, jnp.int32),
            pltpu.VMEM(weight.shape, BF16),
            pltpu.SemaphoreType.DMA((2,)),
        ],
    )
    turned = call(turn_kernel, "turn", shape((patches, TURNED, src, src), BF16), [coupling])
    coupled, give = call(first_kernel, "first", field, [own, *parts, onehot, coupling, turned])
    amps = []
    for step in range(STEPS):
        if step == 0:
            recv, stored = exchange(coupled, give, [own, *parts])
        else:
            (recv,) = exchange(coupled, give)
        if step == STEPS - 1:
            return call(
                last_kernel,
                "last",
                shape((patches, STEPS, src), BF16),
                [recv, incident, self_inverse, *amps],
            )

        def body(*refs, step=step):
            step_kernel(step, *refs)

        coupled, give, amp = call(
            body,
            f"step{step}",
            field + [shape((patches, src), BF16)],
            [recv, incident, self_inverse, lag_table, stored, onehot, coupling, turned, *amps[::-1]],
        )
        amps.append(amp)


def solution(mesh):
    in_specs = (
        P("patch", "slab", None),
        P("patch", None, None),
        P("patch", None, None),
        P("patch", "slab", None, None),
        P("patch", None, None),
        P("patch", None, None),
    )
    out_specs = P("patch", None, None)
    return jax.shard_map(
        on_device, mesh=mesh, in_specs=in_specs, out_specs=out_specs, check_vma=False
    )
```

```python
import functools
import math

import jax
import jax.numpy as jnp
from jax import lax
from jax.experimental import pallas as pl
from jax.experimental.pallas import tpu as pltpu
from jax.sharding import PartitionSpec as P

WMAX = 4
STEPS = 4
LAGS = STEPS - 1
STRIDE = 37
TURNED = 2

BF16 = jnp.bfloat16
F32 = jnp.float32


def dot_f32(a, b, contract):
    return lax.dot_general(a, b, (contract, ((), ())), preferred_element_type=F32)


def spread(values, group, keep):
    out = jnp.where(keep, values, 0.0)
    lanes = out.shape[1]
    step = group
    while step < lanes:
        out = out + pltpu.roll(out, step, 1)
        step *= 2
    return out


def tapped(at, weights):
    found = jnp.where(at == 0, weights[0], 0.0)
    for tap in range(1, WMAX):
        found = jnp.where(at == tap, weights[tap], found)
    return found


def start_copies(pairs, sems):
    copies = [pltpu.make_async_copy(src, dst, sems.at[i]) for i, (src, dst) in enumerate(pairs)]
    for copy in copies:
        copy.start()
    return copies


def history_kernel(plan, table_hbm, weight_hbm, hist_hbm, own_ref, *rest):
    send_refs, (table_ref, weight_ref, hist_ref, sems) = rest[:-4], rest[-4:]
    copies = start_copies(
        [(table_hbm, table_ref), (weight_hbm, weight_ref), (hist_hbm, hist_ref)], sems
    )
    patches, pairs = table_ref.shape[1:]
    _, slab_len, src = hist_ref.shape
    local = own_ref.shape[1] // patches
    slab_id = lax.axis_index("slab")
    lane = lax.broadcasted_iota(jnp.int32, (patches, src), 1)
    turn = lax.rem(src - slab_id * local, src)

    def widen(x):
        return pltpu.roll(jnp.concatenate([x.astype(F32)] * STEPS, axis=1), turn, 1)

    copies[0].wait()
    copies[1].wait()
    first, band = widen(table_ref[1]), widen(table_ref[2])
    wide = weight_ref[...].astype(F32)
    weights = [jnp.where(band > tap, widen(wide[:, tap, :]), 0.0) for tap in range(WMAX)]
    start = first - (lane // pairs + 1 + slab_id * slab_len).astype(F32)

    h = lax.broadcasted_iota(jnp.int32, (slab_len, src), 0).astype(F32)
    copies[2].wait()
    for p in range(0, patches, 2):
        parts = []
        for q in (p, p + 1):
            table = tapped(h - start[q : q + 1], [w[q : q + 1] for w in weights])
            parts.append(dot_f32(table.astype(BF16), hist_ref[q], ((0,), (0,))))
        at = pl.ds(p * local, 2 * local)
        for n in range(STEPS):
            for (s, steps), out_ref in zip(((0, range(STEPS)),) + plan, (own_ref,) + send_refs):
                if n in steps:
                    lo = n * pairs + s * local
                    both = jnp.concatenate([part[lo : lo + local] for part in parts], axis=0)
                    out_ref[n - steps[0], at, :] = both.astype(out_ref.dtype)


def tables_kernel(local, table_hbm, weight_hbm, lag_ref, onehot_ref, table_ref, weight_ref, sems):
    copies = start_copies([(table_hbm, table_ref), (weight_hbm, weight_ref)], sems)
    patches, pairs = table_ref.shape[1:]
    rows = onehot_ref.shape[1]
    slab_id = lax.axis_index("slab")
    core = lax.rem(lax.axis_index("patch"), 2)
    lane = lax.broadcasted_iota(jnp.int32, (patches, rows), 1)
    row = lax.broadcasted_iota(jnp.int32, (patches, rows), 0)
    mine = lane // local == slab_id
    diagonal = lane // local == row
    blank = jnp.zeros((patches, rows - pairs), F32)

    def widen(x):
        return spread(jnp.concatenate([x.astype(F32), blank], axis=1), local, mine)

    for copy in copies:
        copy.wait()
    first, band = widen(table_ref[1]), widen(table_ref[2])
    wide = weight_ref[...].astype(F32)
    weights = [jnp.where(band > tap, widen(wide[:, tap, :]), 0.0) for tap in range(WMAX)]
    lags = [jnp.where(diagonal, tapped(lag - first, weights), 0.0) for lag in range(1, STEPS)]
    for i, lag in enumerate(lags):
        line = jnp.sum(lag, axis=0, keepdims=True)
        lag_ref[i] = jnp.broadcast_to(line, (rows, rows)).T
    obs = table_ref[0]
    obs = (obs // patches % 2 ^ core) * (patches * (lax.axis_size("patch") // 2)) + (
        obs // (2 * patches) * patches + obs % patches
    )
    obs = jnp.sum(jnp.where(diagonal, widen(obs), 0.0), axis=0, keepdims=True).astype(jnp.int32)
    targets = lax.broadcasted_iota(jnp.int32, onehot_ref.shape, 0)
    onehot_ref[...] = jnp.where(targets == obs, 1.0, 0.0).astype(BF16)


def turn_kernel(coup_ref, turned_ref):
    patches, count = turned_ref.shape[:2]
    skip = coup_ref.shape[1] - count
    for p in range(patches):
        for i in range(count):
            turned_ref[p, i] = coup_ref[p, skip + i].astype(F32).T.astype(BF16)


def field_of(driven, onehot_ref, coup_ref, turned_ref, coupled_ref, give_ref):
    rows, src = driven.shape
    patches, local = coup_ref.shape[:2]
    direct = local - turned_ref.shape[1]
    row_id = lax.broadcasted_iota(jnp.int32, (local, src), 0)
    driven = driven.astype(BF16).astype(F32)
    columns = driven.T
    coupled = []
    for p in range(patches):
        mine = driven[p * local : (p + 1) * local].astype(BF16)
        full = dot_f32(mine, coup_ref[p, :direct].reshape(direct * src, src), ((1,), (1,)))
        out = full[:, :src]
        for k in range(1, direct):
            out = jnp.where(row_id == k, full[:, k * src : (k + 1) * src], out)
        for k in range(direct, local):
            r = p * local + k
            terms = turned_ref[p, k - direct].astype(F32) * columns[:, r : r + 1]
            out = jnp.where(row_id == k, jnp.sum(terms, axis=0, keepdims=True), out)
        coupled.append(out)
    coupled = jnp.concatenate(coupled, axis=0).astype(BF16)
    coupled_ref[...] = coupled
    give_ref[...] = dot_f32(onehot_ref[give_ref.shape[0] :], coupled, ((1,), (0,))).astype(BF16)


def keep_kernel(onehot_ref, coupled_ref, keep_ref):
    keep_ref[...] = dot_f32(onehot_ref[: keep_ref.shape[0]], coupled_ref[...], ((1,), (0,)))


def first_kernel(own_ref, *rest):
    part_refs, tail = rest[:-5], rest[-5:]
    driven = own_ref[0]
    for part in part_refs:
        driven = driven + part[0].astype(F32)
    field_of(driven, *tail)


def add_kernel(orders, plan, keep_ref, got_ref, own_ref, *rest):
    part_refs, (send_ref, stored_ref, total_ref) = rest[:-3], rest[-3:]
    join_kernel(orders, keep_ref, got_ref, send_ref, total_ref)
    for n in range(1, STEPS):
        stored = own_ref[n]
        for (_, steps), part in zip(plan, part_refs):
            if n in steps:
                stored = stored + part[n - steps[0]].astype(F32)
        stored_ref[n - 1] = stored


def join_kernel(orders, keep_ref, got_ref, send_ref, total_ref):
    total = (keep_ref[...] + got_ref[...].astype(F32)).astype(BF16)
    total_ref[...] = total.reshape(total_ref.shape)
    core = lax.rem(lax.axis_index("patch"), 2)
    for which, order in enumerate(orders):

        @pl.when(core == which)
        def _(order=order):
            for i, block in enumerate(order):
                send_ref[i] = total_ref[block]


def amplitude_of(step, recv_ref, inc_ref, sinv_ref):
    sources, patches, src = recv_ref.shape
    group = sources // 4
    total = [jnp.sum(recv_ref[i : i + group].astype(F32), axis=0) for i in range(0, sources, group)]
    total = (total[0] + total[1]) + (total[2] + total[3])
    drive = inc_ref[:, step, :] - total
    halves = []
    group = 8
    row_id = lax.broadcasted_iota(jnp.int32, (group, src), 0)
    for p in range(0, patches, group):
        matrices = sinv_ref[p : p + group].reshape(group * src, src)
        full = dot_f32(drive[p : p + group].astype(BF16), matrices, ((1,), (1,)))
        amp = full[:, :src]
        for i in range(1, group):
            amp = jnp.where(row_id == i, full[:, i * src : (i + 1) * src], amp)
        halves.append(amp)
    amp = jnp.concatenate(halves, axis=0)
    return amp.astype(BF16)


def step_kernel(step, recv_ref, inc_ref, sinv_ref, lag_ref, stored_ref, onehot_ref, coup_ref, turned_ref, *rest):
    past_refs, (coupled_ref, give_ref, amp_ref) = rest[:-3], rest[-3:]
    amp = amplitude_of(step, recv_ref, inc_ref, sinv_ref)
    amp_ref[...] = amp
    rows, src = stored_ref.shape[1:]
    patches = amp.shape[0]
    driven = stored_ref[step]
    for lag, past in reversed(list(enumerate([amp] + [r[...] for r in past_refs]))):
        past = past.astype(F32)
        each = [jnp.broadcast_to(past[p : p + 1], (rows // patches, src)) for p in range(patches)]
        driven = driven + lag_ref[lag] * jnp.concatenate(each, axis=0)
    field_of(driven, onehot_ref, coup_ref, turned_ref, coupled_ref, give_ref)


def last_kernel(recv_ref, inc_ref, sinv_ref, *rest):
    past_refs, out_ref = rest[:-1], rest[-1]
    amp = amplitude_of(STEPS - 1, recv_ref, inc_ref, sinv_ref)
    for step, value in enumerate([r[...] for r in past_refs] + [amp]):
        out_ref[:, step, :] = value


def call(kernel, name, outs, args, in_hbm=False, scratch=(), cost=None):
    vmem = pl.BlockSpec(memory_space=pltpu.VMEM)
    space = pltpu.HBM if in_hbm else pltpu.VMEM
    if in_hbm:
        args = [pltpu.with_memory_space_constraint(x, pltpu.HBM) for x in args]
    return pl.pallas_call(
        kernel,
        name=name,
        out_shape=outs,
        in_specs=[pl.BlockSpec(memory_space=space)] * len(args),
        out_specs=jax.tree.map(lambda _: vmem, outs),
        scratch_shapes=scratch,
        cost_estimate=cost,
        compiler_params=pltpu.CompilerParams(vmem_limit_bytes=24 * 2**20),
    )(*args)


def around(n):
    return [i ^ (i >> 1) for i in range(n)]


def on_device(history, interp_weights, pair_table, coupling, self_inverse, incident):
    patches, slab_len, src = history.shape
    local = coupling.shape[1]
    slabs = lax.axis_size("slab")
    blocks = lax.axis_size("patch") // 2
    rows = patches * local
    half = blocks * patches
    cores = [(i, i ^ 1) for i in range(2 * blocks)]
    wide = next(n for n in range(1, blocks + 1) if n * n >= blocks)
    chips = [
        [(y * wide + x, z) for y in around(blocks // wide) for x in around(wide) for z in around(slabs)],
        [(y * wide + x, z) for x in around(wide) for z in around(slabs) for y in around(blocks // wide)],
    ]
    count = len(chips[0])
    chips[0] = [chips[0][i * STRIDE % count] for i in range(count)] if math.gcd(STRIDE, count) == 1 else chips[0]
    groups = [[(2 * b + core) * slabs + z for b, z in chips[core]] for core in range(2)]
    orders = [[b for b, _ in chips[core]] for core in range(2)]

    def exchange(coupled, give, history=None):
        got = lax.ppermute(give, "patch", cores)
        keep = call(keep_kernel, "keep", shape((half, src), F32), [onehot, coupled])
        out = shape((blocks * slabs, patches, src), BF16)
        scratch = [pltpu.VMEM((blocks, patches, src), BF16)]
        if history:
            kernel = functools.partial(add_kernel, orders, plan)
            outs = [out, shape((STEPS - 1, rows, src), F32)]
            send, *stored = call(kernel, "add", outs, [keep, got, *history], scratch=scratch)
        else:
            kernel, stored = functools.partial(join_kernel, orders), []
            send = call(kernel, "join", out, [keep, got], scratch=scratch)
        recv = lax.all_to_all(send, ("patch", "slab"), 0, 0, axis_index_groups=groups, tiled=True)
        return recv, *stored

    shape = jax.ShapeDtypeStruct
    field = [shape((rows, src), BF16), shape((half, src), BF16)]
    table = pair_table.transpose(2, 0, 1)
    weight = interp_weights.transpose(0, 2, 1)
    far = slabs // 2
    order = [far] + [s for s in range(slabs - 1, 0, -1) if s != far]
    plan = tuple((s, range(STEPS)) for s in order)
    own, *sends = call(
        functools.partial(history_kernel, plan),
        "history",
        [
            shape((STEPS, rows, src), F32),
            *(shape((len(steps), rows, src), BF16) for _, steps in plan),
        ],
        [table, weight, history],
        in_hbm=True,
        scratch=[
            pltpu.VMEM(table.shape, jnp.int32),
            pltpu.VMEM(weight.shape, BF16),
            pltpu.VMEM(history.shape, BF16),
            pltpu.SemaphoreType.DMA((3,)),
        ],
        cost=pl.CostEstimate(flops=10**10, bytes_accessed=10**7, transcendentals=0),
    )
    parts = [
        lax.ppermute(x, "slab", [(z, (z + s) % slabs) for z in range(slabs)])
        for (s, _), x in zip(plan, sends)
    ]
    lag_table, onehot = call(
        functools.partial(tables_kernel, local),
        "tables",
        [shape((LAGS, rows, src), F32), shape((2 * half, rows), BF16)],
        [table, weight],
        in_hbm=True,
        scratch=[
            pltpu.VMEM(table.shape, jnp.int32),
            pltpu.VMEM(weight.shape, BF16),
            pltpu.SemaphoreType.DMA((2,)),
        ],
    )
    turned = call(turn_kernel, "turn", shape((patches, TURNED, src, src), BF16), [coupling])
    coupled, give = call(first_kernel, "first", field, [own, *parts, onehot, coupling, turned])
    amps = []
    for step in range(STEPS):
        if step == 0:
            recv, stored = exchange(coupled, give, [own, *parts])
        else:
            (recv,) = exchange(coupled, give)
        if step == STEPS - 1:
            return call(
                last_kernel,
                "last",
                shape((patches, STEPS, src), BF16),
                [recv, incident, self_inverse, *amps],
            )

        def body(*refs, step=step):
            step_kernel(step, *refs)

        coupled, give, amp = call(
            body,
            f"step{step}",
            field + [shape((patches, src), BF16)],
            [recv, incident, self_inverse, lag_table, stored, onehot, coupling, turned, *amps[::-1]],
        )
        amps.append(amp)


def solution(mesh):
    in_specs = (
        P("patch", "slab", None),
        P("patch", None, None),
        P("patch", None, None),
        P("patch", "slab", None, None),
        P("patch", None, None),
        P("patch", None, None),
    )
    out_specs = P("patch", None, None)
    return jax.shard_map(
        on_device, mesh=mesh, in_specs=in_specs, out_specs=out_specs, check_vma=False
    )
```

```python
import functools
import math

import jax
import jax.numpy as jnp
from jax import lax
from jax.experimental import pallas as pl
from jax.experimental.pallas import tpu as pltpu
from jax.sharding import PartitionSpec as P

WMAX = 4
STEPS = 4
LAGS = STEPS - 1
STRIDE = 37
TURNED = 2

BF16 = jnp.bfloat16
F32 = jnp.float32


def dot_f32(a, b, contract):
    return lax.dot_general(a, b, (contract, ((), ())), preferred_element_type=F32)


def spread(values, group, keep):
    out = jnp.where(keep, values, 0.0)
    lanes = out.shape[1]
    step = group
    while step < lanes:
        out = out + pltpu.roll(out, step, 1)
        step *= 2
    return out


def tapped(at, weights):
    found = jnp.where(at == 0, weights[0], 0.0)
    for tap in range(1, WMAX):
        found = jnp.where(at == tap, weights[tap], found)
    return found


def start_copies(pairs, sems):
    copies = [pltpu.make_async_copy(src, dst, sems.at[i]) for i, (src, dst) in enumerate(pairs)]
    for copy in copies:
        copy.start()
    return copies


def history_kernel(plan, table_hbm, weight_hbm, hist_hbm, own_ref, *rest):
    send_refs, (table_ref, weight_ref, hist_ref, sems) = rest[:-4], rest[-4:]
    copies = start_copies(
        [(table_hbm, table_ref), (weight_hbm, weight_ref), (hist_hbm, hist_ref)], sems
    )
    patches, pairs = table_ref.shape[1:]
    _, slab_len, src = hist_ref.shape
    local = own_ref.shape[1] // patches
    slab_id = lax.axis_index("slab")
    lane = lax.broadcasted_iota(jnp.int32, (patches, src), 1)
    turn = lax.rem(src - slab_id * local, src)

    def widen(x):
        return pltpu.roll(jnp.concatenate([x.astype(F32)] * STEPS, axis=1), turn, 1)

    copies[0].wait()
    copies[1].wait()
    first, band = widen(table_ref[1]), widen(table_ref[2])
    wide = weight_ref[...].astype(F32)
    weights = [jnp.where(band > tap, widen(wide[:, tap, :]), 0.0) for tap in range(WMAX)]
    start = first - (lane // pairs + 1 + slab_id * slab_len).astype(F32)

    h = lax.broadcasted_iota(jnp.int32, (slab_len, src), 0).astype(F32)
    copies[2].wait()
    for p in range(0, patches, 2):
        parts = []
        for q in (p, p + 1):
            table = tapped(h - start[q : q + 1], [w[q : q + 1] for w in weights])
            parts.append(dot_f32(table.astype(BF16), hist_ref[q], ((0,), (0,))))
        at = pl.ds(p * local, 2 * local)
        for n in range(STEPS):
            for (s, steps), out_ref in zip(((0, range(STEPS)),) + plan, (own_ref,) + send_refs):
                if n in steps:
                    lo = n * pairs + s * local
                    both = jnp.concatenate([part[lo : lo + local] for part in parts], axis=0)
                    out_ref[n - steps[0], at, :] = both.astype(out_ref.dtype)


def tables_kernel(local, table_hbm, weight_hbm, lag_ref, onehot_ref, table_ref, weight_ref, sems):
    copies = start_copies([(table_hbm, table_ref), (weight_hbm, weight_ref)], sems)
    patches, pairs = table_ref.shape[1:]
    rows = onehot_ref.shape[1]
    slab_id = lax.axis_index("slab")
    core = lax.rem(lax.axis_index("patch"), 2)
    lane = lax.broadcasted_iota(jnp.int32, (patches, rows), 1)
    row = lax.broadcasted_iota(jnp.int32, (patches, rows), 0)
    mine = lane // local == slab_id
    diagonal = lane // local == row
    blank = jnp.zeros((patches, rows - pairs), F32)

    def widen(x):
        return spread(jnp.concatenate([x.astype(F32), blank], axis=1), local, mine)

    for copy in copies:
        copy.wait()
    first, band = widen(table_ref[1]), widen(table_ref[2])
    wide = weight_ref[...].astype(F32)
    weights = [jnp.where(band > tap, widen(wide[:, tap, :]), 0.0) for tap in range(WMAX)]
    lags = [jnp.where(diagonal, tapped(lag - first, weights), 0.0) for lag in range(1, STEPS)]
    for i, lag in enumerate(lags):
        line = jnp.sum(lag, axis=0, keepdims=True)
        lag_ref[i] = jnp.broadcast_to(line, (rows, rows)).T
    obs = table_ref[0]
    obs = (obs // patches % 2 ^ core) * (patches * (lax.axis_size("patch") // 2)) + (
        obs // (2 * patches) * patches + obs % patches
    )
    obs = jnp.sum(jnp.where(diagonal, widen(obs), 0.0), axis=0, keepdims=True).astype(jnp.int32)
    targets = lax.broadcasted_iota(jnp.int32, onehot_ref.shape, 0)
    onehot_ref[...] = jnp.where(targets == obs, 1.0, 0.0).astype(BF16)


def turn_kernel(coup_ref, turned_ref):
    patches, count = turned_ref.shape[:2]
    skip = coup_ref.shape[1] - count
    for p in range(patches):
        for i in range(count):
            turned_ref[p, i] = coup_ref[p, skip + i].astype(F32).T.astype(BF16)


def field_of(driven, onehot_ref, coup_ref, turned_ref, coupled_ref, give_ref):
    rows, src = driven.shape
    patches, local = coup_ref.shape[:2]
    direct = local - turned_ref.shape[1]
    row_id = lax.broadcasted_iota(jnp.int32, (local, src), 0)
    driven = driven.astype(BF16).astype(F32)
    columns = driven.T
    coupled = []
    for p in range(patches):
        mine = driven[p * local : (p + 1) * local].astype(BF16)
        full = dot_f32(mine, coup_ref[p, :direct].reshape(direct * src, src), ((1,), (1,)))
        out = full[:, :src]
        for k in range(1, direct):
            out = jnp.where(row_id == k, full[:, k * src : (k + 1) * src], out)
        for k in range(direct, local):
            r = p * local + k
            terms = turned_ref[p, k - direct].astype(F32) * columns[:, r : r + 1]
            out = jnp.where(row_id == k, jnp.sum(terms, axis=0, keepdims=True), out)
        coupled.append(out)
    coupled = jnp.concatenate(coupled, axis=0).astype(BF16)
    coupled_ref[...] = coupled
    give_ref[...] = dot_f32(onehot_ref[give_ref.shape[0] :], coupled, ((1,), (0,))).astype(BF16)


def keep_kernel(onehot_ref, coupled_ref, keep_ref):
    keep_ref[...] = dot_f32(onehot_ref[: keep_ref.shape[0]], coupled_ref[...], ((1,), (0,)))


def first_kernel(own_ref, *rest):
    part_refs, tail = rest[:-5], rest[-5:]
    driven = own_ref[0]
    for part in part_refs:
        driven = driven + part[0].astype(F32)
    field_of(driven, *tail)


def add_kernel(orders, plan, keep_ref, got_ref, own_ref, *rest):
    part_refs, (send_ref, stored_ref, total_ref) = rest[:-3], rest[-3:]
    join_kernel(orders, keep_ref, got_ref, send_ref, total_ref)
    for n in range(1, STEPS):
        stored = own_ref[n]
        for (_, steps), part in zip(plan, part_refs):
            if n in steps:
                stored = stored + part[n - steps[0]].astype(F32)
        stored_ref[n - 1] = stored


def join_kernel(orders, keep_ref, got_ref, send_ref, total_ref):
    total = (keep_ref[...] + got_ref[...].astype(F32)).astype(BF16)
    total_ref[...] = total.reshape(total_ref.shape)
    core = lax.rem(lax.axis_index("patch"), 2)
    for which, order in enumerate(orders):

        @pl.when(core == which)
        def _(order=order):
            for i, block in enumerate(order):
                send_ref[i] = total_ref[block]


def amplitude_of(step, recv_ref, inc_ref, sinv_ref):
    sources, patches, src = recv_ref.shape
    group = sources // 4
    total = [jnp.sum(recv_ref[i : i + group].astype(F32), axis=0) for i in range(0, sources, group)]
    total = (total[0] + total[1]) + (total[2] + total[3])
    drive = inc_ref[:, step, :] - total
    halves = []
    group = 8
    row_id = lax.broadcasted_iota(jnp.int32, (group, src), 0)
    for p in range(0, patches, group):
        matrices = sinv_ref[p : p + group].reshape(group * src, src)
        full = dot_f32(drive[p : p + group].astype(BF16), matrices, ((1,), (1,)))
        amp = full[:, :src]
        for i in range(1, group):
            amp = jnp.where(row_id == i, full[:, i * src : (i + 1) * src], amp)
        halves.append(amp)
    amp = jnp.concatenate(halves, axis=0)
    return amp.astype(BF16)


def step_kernel(step, recv_ref, inc_ref, sinv_ref, lag_ref, stored_ref, onehot_ref, coup_ref, turned_ref, *rest):
    past_refs, (coupled_ref, give_ref, amp_ref) = rest[:-3], rest[-3:]
    amp = amplitude_of(step, recv_ref, inc_ref, sinv_ref)
    amp_ref[...] = amp
    rows, src = stored_ref.shape[1:]
    patches = amp.shape[0]
    driven = stored_ref[step]
    for lag, past in reversed(list(enumerate([amp] + [r[...] for r in past_refs]))):
        past = past.astype(F32)
        each = [jnp.broadcast_to(past[p : p + 1], (rows // patches, src)) for p in range(patches)]
        driven = driven + lag_ref[lag] * jnp.concatenate(each, axis=0)
    field_of(driven, onehot_ref, coup_ref, turned_ref, coupled_ref, give_ref)


def last_kernel(recv_ref, inc_ref, sinv_ref, *rest):
    past_refs, out_ref = rest[:-1], rest[-1]
    amp = amplitude_of(STEPS - 1, recv_ref, inc_ref, sinv_ref)
    for step, value in enumerate([r[...] for r in past_refs] + [amp]):
        out_ref[:, step, :] = value


def call(kernel, name, outs, args, in_hbm=False, scratch=(), cost=None):
    vmem = pl.BlockSpec(memory_space=pltpu.VMEM)
    space = pltpu.HBM if in_hbm else pltpu.VMEM
    if in_hbm:
        args = [pltpu.with_memory_space_constraint(x, pltpu.HBM) for x in args]
    return pl.pallas_call(
        kernel,
        name=name,
        out_shape=outs,
        in_specs=[pl.BlockSpec(memory_space=space)] * len(args),
        out_specs=jax.tree.map(lambda _: vmem, outs),
        scratch_shapes=scratch,
        cost_estimate=cost,
        compiler_params=pltpu.CompilerParams(vmem_limit_bytes=24 * 2**20),
    )(*args)


def around(n):
    return [i ^ (i >> 1) for i in range(n)]


def on_device(history, interp_weights, pair_table, coupling, self_inverse, incident):
    patches, slab_len, src = history.shape
    local = coupling.shape[1]
    slabs = lax.axis_size("slab")
    blocks = lax.axis_size("patch") // 2
    rows = patches * local
    half = blocks * patches
    cores = [(i, i ^ 1) for i in range(2 * blocks)]
    wide = next(n for n in range(1, blocks + 1) if n * n >= blocks)
    chips = [
        [(y * wide + x, z) for y in around(blocks // wide) for x in around(wide) for z in around(slabs)],
        [(y * wide + x, z) for x in around(wide) for z in around(slabs) for y in around(blocks // wide)],
    ]
    count = len(chips[0])
    chips[0] = [chips[0][i * STRIDE % count] for i in range(count)] if math.gcd(STRIDE, count) == 1 else chips[0]
    groups = [[(2 * b + core) * slabs + z for b, z in chips[core]] for core in range(2)]
    orders = [[b for b, _ in chips[core]] for core in range(2)]

    def exchange(coupled, give, history=None):
        got = lax.ppermute(give, "patch", cores)
        keep = call(keep_kernel, "keep", shape((half, src), F32), [onehot, coupled])
        out = shape((blocks * slabs, patches, src), BF16)
        scratch = [pltpu.VMEM((blocks, patches, src), BF16)]
        if history:
            kernel = functools.partial(add_kernel, orders, plan)
            outs = [out, shape((STEPS - 1, rows, src), F32)]
            send, *stored = call(kernel, "add", outs, [keep, got, *history], scratch=scratch)
        else:
            kernel, stored = functools.partial(join_kernel, orders), []
            send = call(kernel, "join", out, [keep, got], scratch=scratch)
        recv = lax.all_to_all(send, ("patch", "slab"), 0, 0, axis_index_groups=groups, tiled=True)
        return recv, *stored

    shape = jax.ShapeDtypeStruct
    field = [shape((rows, src), BF16), shape((half, src), BF16)]
    table = pair_table.transpose(2, 0, 1)
    weight = interp_weights.transpose(0, 2, 1)
    far = slabs // 2
    order = [far] + [s for s in range(slabs - 1, 0, -1) if s != far]
    plan = tuple((s, range(STEPS)) for s in order)
    own, *sends = call(
        functools.partial(history_kernel, plan),
        "history",
        [
            shape((STEPS, rows, src), F32),
            *(shape((len(steps), rows, src), BF16) for _, steps in plan),
        ],
        [table, weight, history],
        in_hbm=True,
        scratch=[
            pltpu.VMEM(table.shape, jnp.int32),
            pltpu.VMEM(weight.shape, BF16),
            pltpu.VMEM(history.shape, BF16),
            pltpu.SemaphoreType.DMA((3,)),
        ],
    )
    parts = [
        lax.ppermute(x, "slab", [(z, (z + s) % slabs) for z in range(slabs)])
        for (s, _), x in zip(plan, sends)
    ]
    lag_table, onehot = call(
        functools.partial(tables_kernel, local),
        "tables",
        [shape((LAGS, rows, src), F32), shape((2 * half, rows), BF16)],
        [table, weight],
        in_hbm=True,
        scratch=[
            pltpu.VMEM(table.shape, jnp.int32),
            pltpu.VMEM(weight.shape, BF16),
            pltpu.SemaphoreType.DMA((2,)),
        ],
        cost=pl.CostEstimate(flops=10**10, bytes_accessed=10**7, transcendentals=0),
    )
    turned = call(turn_kernel, "turn", shape((patches, TURNED, src, src), BF16), [coupling])
    coupled, give = call(first_kernel, "first", field, [own, *parts, onehot, coupling, turned])
    amps = []
    for step in range(STEPS):
        if step == 0:
            recv, stored = exchange(coupled, give, [own, *parts])
        else:
            (recv,) = exchange(coupled, give)
        if step == STEPS - 1:
            return call(
                last_kernel,
                "last",
                shape((patches, STEPS, src), BF16),
                [recv, incident, self_inverse, *amps],
            )

        def body(*refs, step=step):
            step_kernel(step, *refs)

        coupled, give, amp = call(
            body,
            f"step{step}",
            field + [shape((patches, src), BF16)],
            [recv, incident, self_inverse, lag_table, stored, onehot, coupling, turned, *amps[::-1]],
        )
        amps.append(amp)


def solution(mesh):
    in_specs = (
        P("patch", "slab", None),
        P("patch", None, None),
        P("patch", None, None),
        P("patch", "slab", None, None),
        P("patch", None, None),
        P("patch", None, None),
    )
    out_specs = P("patch", None, None)
    return jax.shard_map(
        on_device, mesh=mesh, in_specs=in_specs, out_specs=out_specs, check_vma=False
    )
```

```python
import functools
import math

import jax
import jax.numpy as jnp
from jax import lax
from jax.experimental import pallas as pl
from jax.experimental.pallas import tpu as pltpu
from jax.sharding import PartitionSpec as P

WMAX = 4
STEPS = 4
LAGS = STEPS - 1
STRIDE = 37
TURNED = 2

BF16 = jnp.bfloat16
F32 = jnp.float32


def dot_f32(a, b, contract):
    return lax.dot_general(a, b, (contract, ((), ())), preferred_element_type=F32)


def spread(values, group, keep):
    out = jnp.where(keep, values, 0.0)
    lanes = out.shape[1]
    step = group
    while step < lanes:
        out = out + pltpu.roll(out, step, 1)
        step *= 2
    return out


def tapped(at, weights):
    found = jnp.where(at == 0, weights[0], 0.0)
    for tap in range(1, WMAX):
        found = jnp.where(at == tap, weights[tap], found)
    return found


def start_copies(pairs, sems):
    copies = [pltpu.make_async_copy(src, dst, sems.at[i]) for i, (src, dst) in enumerate(pairs)]
    for copy in copies:
        copy.start()
    return copies


def history_kernel(plan, table_hbm, weight_hbm, hist_hbm, own_ref, *rest):
    send_refs, (table_ref, weight_ref, hist_ref, sems) = rest[:-4], rest[-4:]
    copies = start_copies(
        [(table_hbm, table_ref), (weight_hbm, weight_ref), (hist_hbm, hist_ref)], sems
    )
    patches, pairs = table_ref.shape[1:]
    _, slab_len, src = hist_ref.shape
    local = own_ref.shape[1] // patches
    slab_id = lax.axis_index("slab")
    lane = lax.broadcasted_iota(jnp.int32, (patches, src), 1)
    turn = lax.rem(src - slab_id * local, src)

    def widen(x):
        return pltpu.roll(jnp.concatenate([x.astype(F32)] * STEPS, axis=1), turn, 1)

    copies[0].wait()
    copies[1].wait()
    first, band = widen(table_ref[1]), widen(table_ref[2])
    wide = weight_ref[...].astype(F32)
    weights = [jnp.where(band > tap, widen(wide[:, tap, :]), 0.0) for tap in range(WMAX)]
    start = first - (lane // pairs + 1 + slab_id * slab_len).astype(F32)

    h = lax.broadcasted_iota(jnp.int32, (slab_len, src), 0).astype(F32)
    copies[2].wait()
    for p in range(0, patches, 2):
        parts = []
        for q in (p, p + 1):
            table = tapped(h - start[q : q + 1], [w[q : q + 1] for w in weights])
            parts.append(dot_f32(table.astype(BF16), hist_ref[q], ((0,), (0,))))
        at = pl.ds(p * local, 2 * local)
        for n in range(STEPS):
            for (s, steps), out_ref in zip(((0, range(STEPS)),) + plan, (own_ref,) + send_refs):
                if n in steps:
                    lo = n * pairs + s * local
                    both = jnp.concatenate([part[lo : lo + local] for part in parts], axis=0)
                    out_ref[n - steps[0], at, :] = both.astype(out_ref.dtype)


def tables_kernel(local, table_hbm, weight_hbm, lag_ref, onehot_ref, table_ref, weight_ref, sems):
    copies = start_copies([(table_hbm, table_ref), (weight_hbm, weight_ref)], sems)
    patches, pairs = table_ref.shape[1:]
    rows = onehot_ref.shape[1]
    slab_id = lax.axis_index("slab")
    core = lax.rem(lax.axis_index("patch"), 2)
    lane = lax.broadcasted_iota(jnp.int32, (patches, rows), 1)
    row = lax.broadcasted_iota(jnp.int32, (patches, rows), 0)
    mine = lane // local == slab_id
    diagonal = lane // local == row
    blank = jnp.zeros((patches, rows - pairs), F32)

    def widen(x):
        return spread(jnp.concatenate([x.astype(F32), blank], axis=1), local, mine)

    for copy in copies:
        copy.wait()
    first, band = widen(table_ref[1]), widen(table_ref[2])
    wide = weight_ref[...].astype(F32)
    weights = [jnp.where(band > tap, widen(wide[:, tap, :]), 0.0) for tap in range(WMAX)]
    lags = [jnp.where(diagonal, tapped(lag - first, weights), 0.0) for lag in range(1, STEPS)]
    for i, lag in enumerate(lags):
        line = jnp.sum(lag, axis=0, keepdims=True)
        lag_ref[i] = jnp.broadcast_to(line, (rows, rows)).T
    obs = table_ref[0]
    obs = (obs // patches % 2 ^ core) * (patches * (lax.axis_size("patch") // 2)) + (
        obs // (2 * patches) * patches + obs % patches
    )
    obs = jnp.sum(jnp.where(diagonal, widen(obs), 0.0), axis=0, keepdims=True).astype(jnp.int32)
    targets = lax.broadcasted_iota(jnp.int32, onehot_ref.shape, 0)
    onehot_ref[...] = jnp.where(targets == obs, 1.0, 0.0).astype(BF16)


def turn_kernel(coup_ref, turned_ref):
    patches, count = turned_ref.shape[:2]
    skip = coup_ref.shape[1] - count
    for p in range(patches):
        for i in range(count):
            turned_ref[p, i] = coup_ref[p, skip + i].astype(F32).T.astype(BF16)


def field_of(driven, onehot_ref, coup_ref, turned_ref, coupled_ref, give_ref):
    rows, src = driven.shape
    patches, local = coup_ref.shape[:2]
    direct = local - turned_ref.shape[1]
    row_id = lax.broadcasted_iota(jnp.int32, (local, src), 0)
    driven = driven.astype(BF16).astype(F32)
    columns = driven.T
    coupled = []
    for p in range(patches):
        mine = driven[p * local : (p + 1) * local].astype(BF16)
        full = dot_f32(mine, coup_ref[p, :direct].reshape(direct * src, src), ((1,), (1,)))
        out = full[:, :src]
        for k in range(1, direct):
            out = jnp.where(row_id == k, full[:, k * src : (k + 1) * src], out)
        for k in range(direct, local):
            r = p * local + k
            terms = turned_ref[p, k - direct].astype(F32) * columns[:, r : r + 1]
            out = jnp.where(row_id == k, jnp.sum(terms, axis=0, keepdims=True), out)
        coupled.append(out)
    coupled = jnp.concatenate(coupled, axis=0).astype(BF16)
    coupled_ref[...] = coupled
    give_ref[...] = dot_f32(onehot_ref[give_ref.shape[0] :], coupled, ((1,), (0,))).astype(BF16)


def keep_kernel(onehot_ref, coupled_ref, keep_ref):
    keep_ref[...] = dot_f32(onehot_ref[: keep_ref.shape[0]], coupled_ref[...], ((1,), (0,)))


def first_kernel(own_ref, *rest):
    part_refs, tail = rest[:-5], rest[-5:]
    driven = own_ref[0]
    for part in part_refs:
        driven = driven + part[0].astype(F32)
    field_of(driven, *tail)


def add_kernel(orders, plan, keep_ref, got_ref, own_ref, *rest):
    part_refs, (send_ref, stored_ref, total_ref) = rest[:-3], rest[-3:]
    join_kernel(orders, keep_ref, got_ref, send_ref, total_ref)
    for n in range(1, STEPS):
        stored = own_ref[n]
        for (_, steps), part in zip(plan, part_refs):
            if n in steps:
                stored = stored + part[n - steps[0]].astype(F32)
        stored_ref[n - 1] = stored


def join_kernel(orders, keep_ref, got_ref, send_ref, total_ref):
    total = (keep_ref[...] + got_ref[...].astype(F32)).astype(BF16)
    total_ref[...] = total.reshape(total_ref.shape)
    core = lax.rem(lax.axis_index("patch"), 2)
    for which, order in enumerate(orders):

        @pl.when(core == which)
        def _(order=order):
            for i, block in enumerate(order):
                send_ref[i] = total_ref[block]


def amplitude_of(step, recv_ref, inc_ref, sinv_ref):
    sources, patches, src = recv_ref.shape
    group = sources // 4
    total = [jnp.sum(recv_ref[i : i + group].astype(F32), axis=0) for i in range(0, sources, group)]
    total = (total[0] + total[1]) + (total[2] + total[3])
    drive = inc_ref[:, step, :] - total
    halves = []
    group = 8
    row_id = lax.broadcasted_iota(jnp.int32, (group, src), 0)
    for p in range(0, patches, group):
        matrices = sinv_ref[p : p + group].reshape(group * src, src)
        full = dot_f32(drive[p : p + group].astype(BF16), matrices, ((1,), (1,)))
        amp = full[:, :src]
        for i in range(1, group):
            amp = jnp.where(row_id == i, full[:, i * src : (i + 1) * src], amp)
        halves.append(amp)
    amp = jnp.concatenate(halves, axis=0)
    return amp.astype(BF16)


def step_kernel(step, recv_ref, inc_ref, sinv_ref, lag_ref, stored_ref, onehot_ref, coup_ref, turned_ref, *rest):
    past_refs, (coupled_ref, give_ref, amp_ref) = rest[:-3], rest[-3:]
    amp = amplitude_of(step, recv_ref, inc_ref, sinv_ref)
    amp_ref[...] = amp
    rows, src = stored_ref.shape[1:]
    patches = amp.shape[0]
    driven = stored_ref[step]
    for lag, past in reversed(list(enumerate([amp] + [r[...] for r in past_refs]))):
        past = past.astype(F32)
        each = [jnp.broadcast_to(past[p : p + 1], (rows // patches, src)) for p in range(patches)]
        driven = driven + lag_ref[lag] * jnp.concatenate(each, axis=0)
    field_of(driven, onehot_ref, coup_ref, turned_ref, coupled_ref, give_ref)


def last_kernel(recv_ref, inc_ref, sinv_ref, *rest):
    past_refs, out_ref = rest[:-1], rest[-1]
    amp = amplitude_of(STEPS - 1, recv_ref, inc_ref, sinv_ref)
    for step, value in enumerate([r[...] for r in past_refs] + [amp]):
        out_ref[:, step, :] = value


def call(kernel, name, outs, args, in_hbm=False, scratch=(), cost=None):
    vmem = pl.BlockSpec(memory_space=pltpu.VMEM)
    space = pltpu.HBM if in_hbm else pltpu.VMEM
    if in_hbm:
        args = [pltpu.with_memory_space_constraint(x, pltpu.HBM) for x in args]
    return pl.pallas_call(
        kernel,
        name=name,
        out_shape=outs,
        in_specs=[pl.BlockSpec(memory_space=space)] * len(args),
        out_specs=jax.tree.map(lambda _: vmem, outs),
        scratch_shapes=scratch,
        cost_estimate=cost,
        compiler_params=pltpu.CompilerParams(vmem_limit_bytes=24 * 2**20),
    )(*args)


def around(n):
    return [i ^ (i >> 1) for i in range(n)]


def on_device(history, interp_weights, pair_table, coupling, self_inverse, incident):
    patches, slab_len, src = history.shape
    local = coupling.shape[1]
    slabs = lax.axis_size("slab")
    blocks = lax.axis_size("patch") // 2
    rows = patches * local
    half = blocks * patches
    cores = [(i, i ^ 1) for i in range(2 * blocks)]
    wide = next(n for n in range(1, blocks + 1) if n * n >= blocks)
    chips = [
        [(y * wide + x, z) for z in around(slabs) for y in around(blocks // wide) for x in around(wide)],
        [(y * wide + x, z) for y in around(blocks // wide) for x in around(wide) for z in around(slabs)],
    ]
    count = len(chips[0])
    chips[0] = [chips[0][i * STRIDE % count] for i in range(count)] if math.gcd(STRIDE, count) == 1 else chips[0]
    groups = [[(2 * b + core) * slabs + z for b, z in chips[core]] for core in range(2)]
    orders = [[b for b, _ in chips[core]] for core in range(2)]

    def exchange(coupled, give, history=None):
        got = lax.ppermute(give, "patch", cores)
        keep = call(keep_kernel, "keep", shape((half, src), F32), [onehot, coupled])
        out = shape((blocks * slabs, patches, src), BF16)
        scratch = [pltpu.VMEM((blocks, patches, src), BF16)]
        if history:
            kernel = functools.partial(add_kernel, orders, plan)
            outs = [out, shape((STEPS - 1, rows, src), F32)]
            send, *stored = call(kernel, "add", outs, [keep, got, *history], scratch=scratch)
        else:
            kernel, stored = functools.partial(join_kernel, orders), []
            send = call(kernel, "join", out, [keep, got], scratch=scratch)
        recv = lax.all_to_all(send, ("patch", "slab"), 0, 0, axis_index_groups=groups, tiled=True)
        return recv, *stored

    shape = jax.ShapeDtypeStruct
    field = [shape((rows, src), BF16), shape((half, src), BF16)]
    table = pair_table.transpose(2, 0, 1)
    weight = interp_weights.transpose(0, 2, 1)
    far = slabs // 2
    order = [far] + [s for s in range(slabs - 1, 0, -1) if s != far]
    plan = tuple((s, range(STEPS)) for s in order)
    own, *sends = call(
        functools.partial(history_kernel, plan),
        "history",
        [
            shape((STEPS, rows, src), F32),
            *(shape((len(steps), rows, src), BF16) for _, steps in plan),
        ],
        [table, weight, history],
        in_hbm=True,
        scratch=[
            pltpu.VMEM(table.shape, jnp.int32),
            pltpu.VMEM(weight.shape, BF16),
            pltpu.VMEM(history.shape, BF16),
            pltpu.SemaphoreType.DMA((3,)),
        ],
    )
    parts = [
        lax.ppermute(x, "slab", [(z, (z + s) % slabs) for z in range(slabs)])
        for (s, _), x in zip(plan, sends)
    ]
    lag_table, onehot = call(
        functools.partial(tables_kernel, local),
        "tables",
        [shape((LAGS, rows, src), F32), shape((2 * half, rows), BF16)],
        [table, weight],
        in_hbm=True,
        scratch=[
            pltpu.VMEM(table.shape, jnp.int32),
            pltpu.VMEM(weight.shape, BF16),
            pltpu.SemaphoreType.DMA((2,)),
        ],
        cost=pl.CostEstimate(flops=10**10, bytes_accessed=10**7, transcendentals=0),
    )
    turned = call(turn_kernel, "turn", shape((patches, TURNED, src, src), BF16), [coupling])
    coupled, give = call(first_kernel, "first", field, [own, *parts, onehot, coupling, turned])
    amps = []
    for step in range(STEPS):
        if step == 0:
            recv, stored = exchange(coupled, give, [own, *parts])
        else:
            (recv,) = exchange(coupled, give)
        if step == STEPS - 1:
            return call(
                last_kernel,
                "last",
                shape((patches, STEPS, src), BF16),
                [recv, incident, self_inverse, *amps],
            )

        def body(*refs, step=step):
            step_kernel(step, *refs)

        coupled, give, amp = call(
            body,
            f"step{step}",
            field + [shape((patches, src), BF16)],
            [recv, incident, self_inverse, lag_table, stored, onehot, coupling, turned, *amps[::-1]],
        )
        amps.append(amp)


def solution(mesh):
    in_specs = (
        P("patch", "slab", None),
        P("patch", None, None),
        P("patch", None, None),
        P("patch", "slab", None, None),
        P("patch", None, None),
        P("patch", None, None),
    )
    out_specs = P("patch", None, None)
    return jax.shard_map(
        on_device, mesh=mesh, in_specs=in_specs, out_specs=out_specs, check_vma=False
    )
```

```python
import functools
import math

import jax
import jax.numpy as jnp
from jax import lax
from jax.experimental import pallas as pl
from jax.experimental.pallas import tpu as pltpu
from jax.sharding import PartitionSpec as P

WMAX = 4
STEPS = 4
LAGS = STEPS - 1
STRIDE = 37
TURNED = 2

BF16 = jnp.bfloat16
F32 = jnp.float32


def dot_f32(a, b, contract):
    return lax.dot_general(a, b, (contract, ((), ())), preferred_element_type=F32)


def spread(values, group, keep):
    out = jnp.where(keep, values, 0.0)
    lanes = out.shape[1]
    step = group
    while step < lanes:
        out = out + pltpu.roll(out, step, 1)
        step *= 2
    return out


def tapped(at, weights):
    found = jnp.where(at == 0, weights[0], 0.0)
    for tap in range(1, WMAX):
        found = jnp.where(at == tap, weights[tap], found)
    return found


def start_copies(pairs, sems):
    copies = [pltpu.make_async_copy(src, dst, sems.at[i]) for i, (src, dst) in enumerate(pairs)]
    for copy in copies:
        copy.start()
    return copies


def history_kernel(plan, table_hbm, weight_hbm, hist_hbm, own_ref, *rest):
    send_refs, (table_ref, weight_ref, hist_ref, sems) = rest[:-4], rest[-4:]
    copies = start_copies(
        [(table_hbm, table_ref), (weight_hbm, weight_ref), (hist_hbm, hist_ref)], sems
    )
    patches, pairs = table_ref.shape[1:]
    _, slab_len, src = hist_ref.shape
    local = own_ref.shape[1] // patches
    slab_id = lax.axis_index("slab")
    lane = lax.broadcasted_iota(jnp.int32, (patches, src), 1)
    turn = lax.rem(src - slab_id * local, src)

    def widen(x):
        return pltpu.roll(jnp.concatenate([x.astype(F32)] * STEPS, axis=1), turn, 1)

    copies[0].wait()
    copies[1].wait()
    first, band = widen(table_ref[1]), widen(table_ref[2])
    wide = weight_ref[...].astype(F32)
    weights = [jnp.where(band > tap, widen(wide[:, tap, :]), 0.0) for tap in range(WMAX)]
    start = first - (lane // pairs + 1 + slab_id * slab_len).astype(F32)

    h = lax.broadcasted_iota(jnp.int32, (slab_len, src), 0).astype(F32)
    copies[2].wait()
    for p in range(0, patches, 2):
        parts = []
        for q in (p, p + 1):
            table = tapped(h - start[q : q + 1], [w[q : q + 1] for w in weights])
            parts.append(dot_f32(table.astype(BF16), hist_ref[q], ((0,), (0,))))
        at = pl.ds(p * local, 2 * local)
        for n in range(STEPS):
            for (s, steps), out_ref in zip(((0, range(STEPS)),) + plan, (own_ref,) + send_refs):
                if n in steps:
                    lo = n * pairs + s * local
                    both = jnp.concatenate([part[lo : lo + local] for part in parts], axis=0)
                    out_ref[n - steps[0], at, :] = both.astype(out_ref.dtype)


def tables_kernel(local, table_hbm, weight_hbm, lag_ref, onehot_ref, table_ref, weight_ref, sems):
    copies = start_copies([(table_hbm, table_ref), (weight_hbm, weight_ref)], sems)
    patches, pairs = table_ref.shape[1:]
    rows = onehot_ref.shape[1]
    slab_id = lax.axis_index("slab")
    core = lax.rem(lax.axis_index("patch"), 2)
    lane = lax.broadcasted_iota(jnp.int32, (patches, rows), 1)
    row = lax.broadcasted_iota(jnp.int32, (patches, rows), 0)
    mine = lane // local == slab_id
    diagonal = lane // local == row
    blank = jnp.zeros((patches, rows - pairs), F32)

    def widen(x):
        return spread(jnp.concatenate([x.astype(F32), blank], axis=1), local, mine)

    for copy in copies:
        copy.wait()
    first, band = widen(table_ref[1]), widen(table_ref[2])
    wide = weight_ref[...].astype(F32)
    weights = [jnp.where(band > tap, widen(wide[:, tap, :]), 0.0) for tap in range(WMAX)]
    lags = [jnp.where(diagonal, tapped(lag - first, weights), 0.0) for lag in range(1, STEPS)]
    for i, lag in enumerate(lags):
        line = jnp.sum(lag, axis=0, keepdims=True)
        lag_ref[i] = jnp.broadcast_to(line, (rows, rows)).T
    obs = table_ref[0]
    obs = (obs // patches % 2 ^ core) * (patches * (lax.axis_size("patch") // 2)) + (
        obs // (2 * patches) * patches + obs % patches
    )
    obs = jnp.sum(jnp.where(diagonal, widen(obs), 0.0), axis=0, keepdims=True).astype(jnp.int32)
    targets = lax.broadcasted_iota(jnp.int32, onehot_ref.shape, 0)
    onehot_ref[...] = jnp.where(targets == obs, 1.0, 0.0).astype(BF16)


def turn_kernel(coup_ref, turned_ref):
    patches, count = turned_ref.shape[:2]
    skip = coup_ref.shape[1] - count
    for p in range(patches):
        for i in range(count):
            turned_ref[p, i] = coup_ref[p, skip + i].astype(F32).T.astype(BF16)


def field_of(driven, onehot_ref, coup_ref, turned_ref, coupled_ref, give_ref):
    rows, src = driven.shape
    patches, local = coup_ref.shape[:2]
    direct = local - turned_ref.shape[1]
    row_id = lax.broadcasted_iota(jnp.int32, (local, src), 0)
    driven = driven.astype(BF16).astype(F32)
    columns = driven.T
    coupled = []
    for p in range(patches):
        mine = driven[p * local : (p + 1) * local].astype(BF16)
        full = dot_f32(mine, coup_ref[p, :direct].reshape(direct * src, src), ((1,), (1,)))
        out = full[:, :src]
        for k in range(1, direct):
            out = jnp.where(row_id == k, full[:, k * src : (k + 1) * src], out)
        for k in range(direct, local):
            r = p * local + k
            terms = turned_ref[p, k - direct].astype(F32) * columns[:, r : r + 1]
            out = jnp.where(row_id == k, jnp.sum(terms, axis=0, keepdims=True), out)
        coupled.append(out)
    coupled = jnp.concatenate(coupled, axis=0).astype(BF16)
    coupled_ref[...] = coupled
    give_ref[...] = dot_f32(onehot_ref[give_ref.shape[0] :], coupled, ((1,), (0,))).astype(BF16)


def keep_kernel(onehot_ref, coupled_ref, keep_ref):
    keep_ref[...] = dot_f32(onehot_ref[: keep_ref.shape[0]], coupled_ref[...], ((1,), (0,)))


def first_kernel(own_ref, *rest):
    part_refs, tail = rest[:-5], rest[-5:]
    driven = own_ref[0]
    for part in part_refs:
        driven = driven + part[0].astype(F32)
    field_of(driven, *tail)


def add_kernel(orders, plan, keep_ref, got_ref, own_ref, *rest):
    part_refs, (send_ref, stored_ref, total_ref) = rest[:-3], rest[-3:]
    join_kernel(orders, keep_ref, got_ref, send_ref, total_ref)
    for n in range(1, STEPS):
        stored = own_ref[n]
        for (_, steps), part in zip(plan, part_refs):
            if n in steps:
                stored = stored + part[n - steps[0]].astype(F32)
        stored_ref[n - 1] = stored


def join_kernel(orders, keep_ref, got_ref, send_ref, total_ref):
    total = (keep_ref[...] + got_ref[...].astype(F32)).astype(BF16)
    total_ref[...] = total.reshape(total_ref.shape)
    core = lax.rem(lax.axis_index("patch"), 2)
    for which, order in enumerate(orders):

        @pl.when(core == which)
        def _(order=order):
            for i, block in enumerate(order):
                send_ref[i] = total_ref[block]


def amplitude_of(step, recv_ref, inc_ref, sinv_ref):
    sources, patches, src = recv_ref.shape
    group = sources // 8
    total = [jnp.sum(recv_ref[i : i + group].astype(F32), axis=0) for i in range(0, sources, group)]
    while len(total) > 1:
        total = [a + b for a, b in zip(total[::2], total[1::2])]
    total = total[0]
    drive = inc_ref[:, step, :] - total
    halves = []
    group = 8
    row_id = lax.broadcasted_iota(jnp.int32, (group, src), 0)
    for p in range(0, patches, group):
        matrices = sinv_ref[p : p + group].reshape(group * src, src)
        full = dot_f32(drive[p : p + group].astype(BF16), matrices, ((1,), (1,)))
        amp = full[:, :src]
        for i in range(1, group):
            amp = jnp.where(row_id == i, full[:, i * src : (i + 1) * src], amp)
        halves.append(amp)
    amp = jnp.concatenate(halves, axis=0)
    return amp.astype(BF16)


def step_kernel(step, recv_ref, inc_ref, sinv_ref, lag_ref, stored_ref, onehot_ref, coup_ref, turned_ref, *rest):
    past_refs, (coupled_ref, give_ref, amp_ref) = rest[:-3], rest[-3:]
    amp = amplitude_of(step, recv_ref, inc_ref, sinv_ref)
    amp_ref[...] = amp
    rows, src = stored_ref.shape[1:]
    patches = amp.shape[0]
    driven = stored_ref[step]
    for lag, past in reversed(list(enumerate([amp] + [r[...] for r in past_refs]))):
        past = past.astype(F32)
        each = [jnp.broadcast_to(past[p : p + 1], (rows // patches, src)) for p in range(patches)]
        driven = driven + lag_ref[lag] * jnp.concatenate(each, axis=0)
    field_of(driven, onehot_ref, coup_ref, turned_ref, coupled_ref, give_ref)


def last_kernel(recv_ref, inc_ref, sinv_ref, *rest):
    past_refs, out_ref = rest[:-1], rest[-1]
    amp = amplitude_of(STEPS - 1, recv_ref, inc_ref, sinv_ref)
    for step, value in enumerate([r[...] for r in past_refs] + [amp]):
        out_ref[:, step, :] = value


def call(kernel, name, outs, args, in_hbm=False, scratch=(), cost=None):
    vmem = pl.BlockSpec(memory_space=pltpu.VMEM)
    space = pltpu.HBM if in_hbm else pltpu.VMEM
    if in_hbm:
        args = [pltpu.with_memory_space_constraint(x, pltpu.HBM) for x in args]
    return pl.pallas_call(
        kernel,
        name=name,
        out_shape=outs,
        in_specs=[pl.BlockSpec(memory_space=space)] * len(args),
        out_specs=jax.tree.map(lambda _: vmem, outs),
        scratch_shapes=scratch,
        cost_estimate=cost,
        compiler_params=pltpu.CompilerParams(vmem_limit_bytes=24 * 2**20),
    )(*args)


def around(n):
    return [i ^ (i >> 1) for i in range(n)]


def on_device(history, interp_weights, pair_table, coupling, self_inverse, incident):
    patches, slab_len, src = history.shape
    local = coupling.shape[1]
    slabs = lax.axis_size("slab")
    blocks = lax.axis_size("patch") // 2
    rows = patches * local
    half = blocks * patches
    cores = [(i, i ^ 1) for i in range(2 * blocks)]
    wide = next(n for n in range(1, blocks + 1) if n * n >= blocks)
    chips = [
        [(y * wide + x, z) for z in around(slabs) for y in around(blocks // wide) for x in around(wide)],
        [(y * wide + x, z) for y in around(blocks // wide) for x in around(wide) for z in around(slabs)],
    ]
    count = len(chips[0])
    chips[0] = [chips[0][i * STRIDE % count] for i in range(count)] if math.gcd(STRIDE, count) == 1 else chips[0]
    groups = [[(2 * b + core) * slabs + z for b, z in chips[core]] for core in range(2)]
    orders = [[b for b, _ in chips[core]] for core in range(2)]

    def exchange(coupled, give, history=None):
        got = lax.ppermute(give, "patch", cores)
        keep = call(keep_kernel, "keep", shape((half, src), F32), [onehot, coupled])
        out = shape((blocks * slabs, patches, src), BF16)
        scratch = [pltpu.VMEM((blocks, patches, src), BF16)]
        if history:
            kernel = functools.partial(add_kernel, orders, plan)
            outs = [out, shape((STEPS - 1, rows, src), F32)]
            send, *stored = call(kernel, "add", outs, [keep, got, *history], scratch=scratch)
        else:
            kernel, stored = functools.partial(join_kernel, orders), []
            send = call(kernel, "join", out, [keep, got], scratch=scratch)
        recv = lax.all_to_all(send, ("patch", "slab"), 0, 0, axis_index_groups=groups, tiled=True)
        return recv, *stored

    shape = jax.ShapeDtypeStruct
    field = [shape((rows, src), BF16), shape((half, src), BF16)]
    table = pair_table.transpose(2, 0, 1)
    weight = interp_weights.transpose(0, 2, 1)
    far = slabs // 2
    order = [far] + [s for s in range(slabs - 1, 0, -1) if s != far]
    plan = tuple((s, range(STEPS)) for s in order)
    own, *sends = call(
        functools.partial(history_kernel, plan),
        "history",
        [
            shape((STEPS, rows, src), F32),
            *(shape((len(steps), rows, src), BF16) for _, steps in plan),
        ],
        [table, weight, history],
        in_hbm=True,
        scratch=[
            pltpu.VMEM(table.shape, jnp.int32),
            pltpu.VMEM(weight.shape, BF16),
            pltpu.VMEM(history.shape, BF16),
            pltpu.SemaphoreType.DMA((3,)),
        ],
    )
    parts = [
        lax.ppermute(x, "slab", [(z, (z + s) % slabs) for z in range(slabs)])
        for (s, _), x in zip(plan, sends)
    ]
    lag_table, onehot = call(
        functools.partial(tables_kernel, local),
        "tables",
        [shape((LAGS, rows, src), F32), shape((2 * half, rows), BF16)],
        [table, weight],
        in_hbm=True,
        scratch=[
            pltpu.VMEM(table.shape, jnp.int32),
            pltpu.VMEM(weight.shape, BF16),
            pltpu.SemaphoreType.DMA((2,)),
        ],
        cost=pl.CostEstimate(flops=10**10, bytes_accessed=10**7, transcendentals=0),
    )
    turned = call(turn_kernel, "turn", shape((patches, TURNED, src, src), BF16), [coupling])
    coupled, give = call(first_kernel, "first", field, [own, *parts, onehot, coupling, turned])
    amps = []
    for step in range(STEPS):
        if step == 0:
            recv, stored = exchange(coupled, give, [own, *parts])
        else:
            (recv,) = exchange(coupled, give)
        if step == STEPS - 1:
            return call(
                last_kernel,
                "last",
                shape((patches, STEPS, src), BF16),
                [recv, incident, self_inverse, *amps],
            )

        def body(*refs, step=step):
            step_kernel(step, *refs)

        coupled, give, amp = call(
            body,
            f"step{step}",
            field + [shape((patches, src), BF16)],
            [recv, incident, self_inverse, lag_table, stored, onehot, coupling, turned, *amps[::-1]],
        )
        amps.append(amp)


def solution(mesh):
    in_specs = (
        P("patch", "slab", None),
        P("patch", None, None),
        P("patch", None, None),
        P("patch", "slab", None, None),
        P("patch", None, None),
        P("patch", None, None),
    )
    out_specs = P("patch", None, None)
    return jax.shard_map(
        on_device, mesh=mesh, in_specs=in_specs, out_specs=out_specs, check_vma=False
    )
```
